512 devices in a mesh: member: 32 (over z_hi, x, core), fsdp: 16 (over y, z_lo).
Axes of the slice: x: 4, y: 8, z: 8 (z_hi: 4, z_lo: 2; z = z_hi * 2 + z_lo), core: 2. Of those that a mesh axis runs over, the one named last changes fastest.
Arguments:
- attention_out: bfloat16 [32, 2048, 2048], P('member', 'fsdp'), may hold values from -6 to 6
- residual: bfloat16 [32, 2048, 2048], P('member', 'fsdp'), may hold values from -6 to 6
- upstream: bfloat16 [32, 2048, 2048], P('member', 'fsdp'), may hold values from -6 to 6
- norm_gain: bfloat16 [32, 2048], P('member', 'fsdp'), may hold values from 0.099609375 to 1.8984375
- weight: bfloat16 [32, 2048, 2048], P('member', None, 'fsdp'), may hold values from -6 to 6
- first_moment: bfloat16 [32, 2048, 2048], P('member', None, 'fsdp'), may hold values from -4 to 4
- second_moment: bfloat16 [32, 2048, 2048], P('member', None, 'fsdp'), may hold values from 0.049804688 to 2
- sources: int32 [32], replicated, may hold values from 0 to 31, as said below
- rate_index: int32 [32], P('member'), may hold values from 0 to 4
Outputs:
- new_weight: bfloat16 [32, 2048, 2048], P('member', None, 'fsdp')
- new_first: bfloat16 [32, 2048, 2048], P('member', None, 'fsdp')
- new_second: bfloat16 [32, 2048, 2048], P('member', None, 'fsdp')
The draws below stay inside these ranges and needn't reach their ends.
Inputs may be any that keep to these rules, and one draw needn't show every extreme that they name: `sources`: 8 members take the state of as many distinct other members, which keep their own; every other member names itself.
All inputs are finite; a program needn't handle non-finite values.
Results may differ from the reference program's by a relative error of at most 0.005.
Values may be sent and summed in bfloat16 or wider, within the bound.
No kernel may reach another device: no remote copies, remote signals or barrier semaphores. Data moves between devices by JAX's collectives and lax.ppermute only.
A program may use at most 64 MiB of HBM per device.

```python
import math
import jax
import jax.numpy as jnp
from jax import lax

D = 2048
HEADS = 16
HEAD_DIM = 128
MEMBERS = 32
TOKENS = 2048


def shared_parts(key):
    head_dirs = jax.random.normal(jax.random.fold_in(key, 101), (HEADS * HEAD_DIM,), jnp.float32)
    feature_dirs = jax.random.normal(jax.random.fold_in(key, 102), (D,), jnp.float32)
    token_loads = jax.random.normal(jax.random.fold_in(key, 103), (MEMBERS, TOKENS), jnp.float32)
    return (head_dirs, feature_dirs, token_loads)


def draw_sources(key, part):
    key = jax.random.fold_in(key, 7)
    ranking = jax.random.permutation(key, MEMBERS).astype(jnp.int32)
    quarter = MEMBERS // 4
    positions = jnp.arange(MEMBERS, dtype=jnp.int32)
    partner = ranking[MEMBERS - 1 - positions]
    chosen = jnp.where(positions < quarter, partner, ranking)
    return jnp.zeros((MEMBERS,), jnp.int32).at[ranking].set(chosen)


def draw_attention_out(key, part):
    head_dirs, feature_dirs, token_loads = shared_parts(key)
    key = jax.random.fold_in(key, 11)
    shape = (MEMBERS, TOKENS, HEADS * HEAD_DIM)
    base_noise = jax.random.normal(key, shape, jnp.float32)
    values = 0.8 * base_noise + 0.6 * token_loads[:, :, None] * head_dirs[None, None, :]
    return jnp.clip(values, -6.0, 6.0).astype(jnp.bfloat16)


def draw_residual(key, part):
    head_dirs, feature_dirs, token_loads = shared_parts(key)
    key = jax.random.fold_in(key, 12)
    shape = (MEMBERS, TOKENS, D)
    base_noise = jax.random.normal(key, shape, jnp.float32)
    values = 0.5 * base_noise + 0.9 * token_loads[:, :, None] * feature_dirs[None, None, :]
    return jnp.clip(values, -6.0, 6.0).astype(jnp.bfloat16)


def draw_upstream(key, part):
    head_dirs, feature_dirs, token_loads = shared_parts(key)
    key = jax.random.fold_in(key, 13)
    shape = (MEMBERS, TOKENS, D)
    other_loads = jax.random.normal(jax.random.fold_in(key, 2), (MEMBERS, TOKENS), jnp.float32)
    base_noise = jax.random.normal(key, shape, jnp.float32)
    values = 0.6 * base_noise + 0.7 * other_loads[:, :, None] * feature_dirs[None, None, :]
    return jnp.clip(values, -6.0, 6.0).astype(jnp.bfloat16)


def draw_weight(key, part):
    head_dirs, feature_dirs, token_loads = shared_parts(key)
    key = jax.random.fold_in(key, 14)
    shape = (MEMBERS, HEADS * HEAD_DIM, D)
    common = 1.0 / (0.6 * math.sqrt(HEADS * HEAD_DIM))
    base_noise = jax.random.normal(key, shape, jnp.float32)
    values = 0.8 * base_noise + common * head_dirs[None, :, None] * feature_dirs[None, None, :]
    return jnp.clip(values, -6.0, 6.0).astype(jnp.bfloat16)


def place_ends(array, rng, low, largest):
    longest = array.shape.index(max(array.shape))
    spots = []
    for shift in (0, 1):
        where = [jax.random.randint(jax.random.fold_in(rng, axis), (), 0, length) for axis, length in enumerate(array.shape)]
        where[longest] = (where[longest] + shift) % array.shape[longest]
        spots.append(tuple(where))
    return array.at[spots[0]].set(low).at[spots[1]].set(largest)


def steps_of(stream_key, dims, pieces, low, high):
    loudness, own = 1.0, jax.random.fold_in(stream_key, 6)
    for position, shards_of in pieces:
        steps = jnp.exp(jax.random.uniform(jax.random.fold_in(own, position), (shards_of,), jnp.float32, low / len(pieces), high / len(pieces)))
        loudness = loudness * jnp.repeat(steps, dims[position] // shards_of).reshape([-1 if axis == position else 1 for axis in range(len(dims))])
    return loudness


def bell_draw(key, dims, deviation, reach, pieces=(), held_as=jnp.bfloat16):
    entries = jax.random.normal(key, dims, jnp.float32) * deviation
    if len(pieces) > 0:
        entries = steps_of(key, dims, pieces, -0.22, 0.18) * entries
    return jnp.clip(entries, min=-reach, max=reach).astype(held_as)


def setup_inputs(seed: int = 0) -> dict:
    arg_keys = jax.random.split(jax.random.key(seed), 10)
    attention_out = draw_attention_out(jax.random.fold_in(arg_keys[9], 71), 0)
    residual = draw_residual(jax.random.fold_in(arg_keys[9], 71), 0)
    upstream = draw_upstream(jax.random.fold_in(arg_keys[9], 71), 0)
    norm_gain = jnp.clip(1.0 + 0.18 * jax.random.normal(arg_keys[3], (MEMBERS, D), jnp.float32), 0.099609375, 1.8984375).astype(jnp.bfloat16)
    weight = draw_weight(jax.random.fold_in(arg_keys[9], 71), 0)
    first_moment = bell_draw(arg_keys[5], (MEMBERS, HEADS * HEAD_DIM, D), 0.3, 4.0, ((0, 32), (2, 16)))
    second_moment = jnp.clip(jnp.exp(math.log(2.0) - 3.6927934 * jax.random.uniform(arg_keys[6], (MEMBERS, HEADS * HEAD_DIM, D), jnp.float32) ** steps_of(arg_keys[6], (MEMBERS, HEADS * HEAD_DIM, D), ((0, 32), (2, 16)), -0.2, 0.2)), 0.049804688, 2.0).astype(jnp.bfloat16)
    sources = draw_sources(jax.random.fold_in(arg_keys[9], 71), 0)
    rate_index = place_ends(jax.random.randint(arg_keys[8], (MEMBERS,), 0, 5), jax.random.fold_in(arg_keys[8], 1), 0, 4).astype(jnp.int32)
    return dict(attention_out=attention_out, residual=residual, upstream=upstream, norm_gain=norm_gain, weight=weight, first_moment=first_moment, second_moment=second_moment, sources=sources, rate_index=rate_index)


EPS = 1e-06
ADAM_EPS = 1e-08
BETA_ONE = 0.9
BETA_TWO = 0.95
DECAY = 0.1
bias_one = 1.0 - 0.9 ** 10
bias_two = 1.0 - 0.95 ** 10
RATE_TABLE = (0.02, 0.032, 0.05, 0.08, 0.125)

def member_step(attention_rows, residual_rows, upstream_rows, gain_row, weight_now, first_now, second_now, rate_slot):
    inv_scale = 1.0 / math.sqrt(weight_now.shape[0])
    linear = jnp.dot(attention_rows.astype(jnp.float32), weight_now.astype(jnp.float32))
    hidden_sum = residual_rows.astype(jnp.float32) + linear * inv_scale
    feature_count = hidden_sum.shape[1]
    squares = lax.optimization_barrier(jnp.sum(hidden_sum * hidden_sum, axis=1, keepdims=True))
    scaled = upstream_rows.astype(jnp.float32) * gain_row.astype(jnp.float32)[None, :]
    inner_sums = lax.optimization_barrier(jnp.sum(scaled * hidden_sum, axis=1, keepdims=True))
    inverse = lax.rsqrt(squares / feature_count + EPS)
    delta_rows = (scaled * inverse - hidden_sum * (inner_sums / feature_count) * inverse ** 3).astype(jnp.bfloat16)
    gradient = jnp.dot(attention_rows.astype(jnp.float32).T, delta_rows.astype(jnp.float32)) * inv_scale
    rate_table = jnp.asarray(RATE_TABLE, dtype=jnp.float32)
    rate_value = jnp.sum(jnp.where(jnp.arange(5) == rate_slot, rate_table, 0.0))
    first_sum = BETA_ONE * first_now.astype(jnp.float32) + (1.0 - BETA_ONE) * gradient
    second_sum = BETA_TWO * second_now.astype(jnp.float32) + (1.0 - BETA_TWO) * gradient * gradient
    update = first_sum / bias_one / (jnp.sqrt(second_sum / bias_two) + ADAM_EPS)
    weight_new = weight_now.astype(jnp.float32) * (1.0 - rate_value * DECAY) - rate_value * update
    return (weight_new.astype(jnp.bfloat16), first_sum.astype(jnp.bfloat16), second_sum.astype(jnp.bfloat16))

def member_call(packed):
    return member_step(*packed)

def reference(attention_out, residual, upstream, norm_gain, weight, first_moment, second_moment, sources, rate_index):
    copied_weight = weight[sources]
    copied_first = first_moment[sources]
    copied_second = second_moment[sources]
    results = lax.map(member_call, (attention_out, residual, upstream, norm_gain, copied_weight, copied_first, copied_second, rate_index))
    return (results[0], results[1], results[2])
```

```python
import math

import jax
import jax.numpy as jnp
from jax import lax
from jax.sharding import Mesh
from jax.sharding import PartitionSpec as P

EPS = 1e-06
ADAM_EPS = 1e-08
BETA_ONE = 0.9
BETA_TWO = 0.95
DECAY = 0.1
bias_one = 1.0 - 0.9**10
bias_two = 1.0 - 0.95**10
RATE_TABLE = (0.02, 0.032, 0.05, 0.08, 0.125)
MINOR = 2


def adamw_update(weight_now, first_now, second_now, gradient, rate_value):
    first_sum = BETA_ONE * first_now.astype(jnp.float32) + (1.0 - BETA_ONE) * gradient
    second_sum = BETA_TWO * second_now.astype(jnp.float32) + (1.0 - BETA_TWO) * gradient * gradient
    update = first_sum / bias_one / (jnp.sqrt(second_sum / bias_two) + ADAM_EPS)
    weight_new = weight_now.astype(jnp.float32) * (1.0 - rate_value * DECAY) - rate_value * update
    return (
        weight_new.astype(jnp.bfloat16),
        first_sum.astype(jnp.bfloat16),
        second_sum.astype(jnp.bfloat16),
    )


def swap_minor(array):
    return lax.ppermute(array, "minor", [(0, 1), (1, 0)])


def sum_over_major(array):
    size = lax.axis_size("major")
    total = array
    parts = [
        lax.ppermute(array, "major", [(i, (i + shift) % size) for i in range(size)])
        for shift in range(1, size)
    ]
    for part in parts:
        total = total + part
    return total


def exchange(array, sources):
    out = lax.all_to_all(array, "member", split_axis=0, concat_axis=0, tiled=True)
    return lax.all_to_all(out[sources], "member", split_axis=0, concat_axis=0, tiled=True)


def local(
    attention_out,
    residual,
    upstream,
    norm_gain,
    weight,
    first_moment,
    second_moment,
    sources,
    rate_index,
):
    members = lax.axis_size("member")
    major = lax.axis_size("major")
    minor = lax.axis_index("minor")
    depth, width = weight.shape[1:]
    rows = depth // members
    tokens, features = residual.shape[1:]
    block = features // major

    weight_here = exchange(weight[0].reshape(members, rows, width), sources)
    moments = jnp.stack(
        (first_moment[0].reshape(members, rows, width), second_moment[0].reshape(members, rows, width)),
        axis=1,
    )
    moments = exchange(moments, sources)
    weight_here = weight_here.reshape(depth, width)
    first_here = moments[:, 0].reshape(depth, width)
    second_here = moments[:, 1].reshape(depth, width)

    gathered = lax.all_gather(attention_out[0], "major", axis=0, tiled=True)
    stream = jnp.stack(
        (
            residual[0].reshape(tokens, major, block).transpose(1, 0, 2),
            upstream[0].reshape(tokens, major, block).transpose(1, 0, 2),
        ),
        axis=1,
    )
    stream = lax.all_to_all(stream, "major", split_axis=0, concat_axis=0, tiled=True)
    resid_cols = stream[:, 0].reshape(major * tokens, block)
    upstream_cols = stream[:, 1].reshape(major * tokens, block)

    gain_other = swap_minor(norm_gain[0])
    weight_other = swap_minor(weight_here)
    first_half = minor == 0
    gain = jnp.where(
        first_half,
        jnp.concatenate((norm_gain[0], gain_other)),
        jnp.concatenate((gain_other, norm_gain[0])),
    )
    weight_both = jnp.where(
        first_half,
        jnp.concatenate((weight_here, weight_other), axis=1),
        jnp.concatenate((weight_other, weight_here), axis=1),
    )

    inv_scale = 1.0 / math.sqrt(depth)
    linear = jnp.dot(gathered, weight_both, preferred_element_type=jnp.float32)
    hidden_sum = resid_cols.astype(jnp.float32) + linear * inv_scale
    scaled = upstream_cols.astype(jnp.float32) * gain.astype(jnp.float32)[None, :]
    sums = jnp.stack(
        (jnp.sum(hidden_sum * hidden_sum, axis=1), jnp.sum(scaled * hidden_sum, axis=1))
    )
    sums = sum_over_major(sums)
    inverse = lax.rsqrt(sums[0] / features + EPS)
    factor = (sums[1] / features * inverse * inverse * inverse)[:, None]
    delta = (scaled * inverse[:, None] - hidden_sum * factor).astype(jnp.bfloat16)
    partial = (
        lax.dot_general(
            gathered, delta, (((0,), (0,)), ((), ())), preferred_element_type=jnp.float32
        )
        * inv_scale
    )
    low, high = partial[:, :width], partial[:, width:]
    mine = jnp.where(first_half, low, high)
    theirs = jnp.where(first_half, high, low).astype(jnp.bfloat16)
    gradient = mine + swap_minor(theirs).astype(jnp.float32)

    rate_table = jnp.asarray(RATE_TABLE, dtype=jnp.float32)
    rate_value = jnp.sum(jnp.where(jnp.arange(5) == rate_index[0], rate_table, 0.0))
    weight_new, first_new, second_new = adamw_update(
        weight_here, first_here, second_here, gradient, rate_value
    )
    return (weight_new[None], first_new[None], second_new[None])


def solution(mesh):
    members, shards = mesh.devices.shape
    split = Mesh(mesh.devices.reshape(members, shards // MINOR, MINOR), ("member", "major", "minor"))
    fsdp = ("major", "minor")
    in_specs = (
        P("member", fsdp, None),
        P("member", fsdp, None),
        P("member", fsdp, None),
        P("member", fsdp),
        P("member", None, fsdp),
        P("member", None, fsdp),
        P("member", None, fsdp),
        P(),
        P("member"),
    )
    out_specs = (P("member", None, fsdp),) * 3
    return jax.shard_map(local, mesh=split, in_specs=in_specs, out_specs=out_specs, check_vma=False)
```

```python
import functools
import math

import jax
import jax.numpy as jnp
from jax import lax
from jax.experimental import pallas as pl
from jax.experimental.pallas import tpu as pltpu
from jax.sharding import Mesh
from jax.sharding import PartitionSpec as P

EPS = 1e-06
ADAM_EPS = 1e-08
BETA_ONE = 0.9
BETA_TWO = 0.95
DECAY = 0.1
bias_one = 1.0 - 0.9**10
bias_two = 1.0 - 0.95**10
RATE_TABLE = (0.02, 0.032, 0.05, 0.08, 0.125)
MINOR = 2
LANES = 128
VMEM_LIMIT = 24 * 1024 * 1024


def adamw_update(weight_now, first_now, second_now, gradient, rate_value):
    first_sum = BETA_ONE * first_now.astype(jnp.float32) + (1.0 - BETA_ONE) * gradient
    second_sum = BETA_TWO * second_now.astype(jnp.float32) + (1.0 - BETA_TWO) * gradient * gradient
    update = first_sum / bias_one / (jnp.sqrt(second_sum / bias_two) + ADAM_EPS)
    weight_new = weight_now.astype(jnp.float32) * (1.0 - rate_value * DECAY) - rate_value * update
    return (
        weight_new.astype(jnp.bfloat16),
        first_sum.astype(jnp.bfloat16),
        second_sum.astype(jnp.bfloat16),
    )


def forward_kernel(inv_scale, minor_ref, rows_ref, own_ref, other_ref, stream_ref, gain_ref, hidden_ref, sums_ref, both_ref):
    width = own_ref.shape[1]

    @pl.when(pl.program_id(0) == 0)
    def _():
        @pl.when(minor_ref[0] == 0)
        def _():
            both_ref[:, :width] = own_ref[...]
            both_ref[:, width:] = other_ref[...]

        @pl.when(minor_ref[0] != 0)
        def _():
            both_ref[:, :width] = other_ref[...]
            both_ref[:, width:] = own_ref[...]

    linear = jnp.dot(rows_ref[...], both_ref[...], preferred_element_type=jnp.float32)
    count = rows_ref.shape[0]
    stream = stream_ref[...]
    resid = stream[:, 0].reshape(count, 2 * width).astype(jnp.float32)
    upstream = stream[:, 1].reshape(count, 2 * width).astype(jnp.float32)
    hidden = resid + linear * inv_scale
    hidden_ref[...] = hidden
    scaled = upstream * gain_ref[...]
    squares = jnp.sum(hidden * hidden, axis=1, keepdims=True)
    inner = jnp.sum(scaled * hidden, axis=1, keepdims=True)
    lane = lax.broadcasted_iota(jnp.int32, (count, LANES), 1)
    packed = jnp.where(lane == 0, squares, jnp.where(lane == 1, inner, 0.0))
    sums_ref[...] = packed.T[: sums_ref.shape[0]]


def forward(minor, rows, own, other, stream, gain, inv_scale):
    tokens, depth = rows.shape
    width = own.shape[1]
    per = stream.shape[2]
    step = 2 * per
    return pl.pallas_call(
        functools.partial(forward_kernel, inv_scale),
        grid_spec=pltpu.PrefetchScalarGridSpec(
            num_scalar_prefetch=1,
            grid=(tokens // step,),
            in_specs=[
                pl.BlockSpec((step, depth), lambda i, m: (i, 0)),
                pl.BlockSpec((depth, width), lambda i, m: (0, 0)),
                pl.BlockSpec((depth, width), lambda i, m: (0, 0)),
                pl.BlockSpec((2, 2, per, 2 * width), lambda i, m: (i, 0, 0, 0)),
                pl.BlockSpec((1, 2 * width), lambda i, m: (0, 0)),
            ],
            out_specs=[
                pl.BlockSpec((step, 2 * width), lambda i, m: (i, 0)),
                pl.BlockSpec((8, step), lambda i, m: (0, i)),
            ],
            scratch_shapes=[pltpu.VMEM((depth, 2 * width), jnp.bfloat16)],
        ),
        out_shape=[
            jax.ShapeDtypeStruct((tokens, 2 * width), jnp.float32),
            jax.ShapeDtypeStruct((8, tokens), jnp.float32),
        ],
        compiler_params=pltpu.CompilerParams(vmem_limit_bytes=VMEM_LIMIT),
        cost_estimate=pl.CostEstimate(
            flops=4 * tokens * depth * width, bytes_accessed=7 * 1024 * 1024, transcendentals=0
        ),
        name="forward",
    )(minor, rows, own, other, stream, gain)


def backward_kernel(inv_scale, features, minor_ref, rows_ref, hidden_ref, stream_ref, gain_ref, sums_ref, mine_ref, theirs_ref, delta_ref):
    width = mine_ref.shape[1]
    tokens = hidden_ref.shape[0]
    blocks, _, per, _ = stream_ref.shape

    @pl.when(pl.program_id(0) == 0)
    def _():
        squares = sums_ref[0:1, :]
        inner = sums_ref[1:2, :]
        inverse = lax.rsqrt(squares / features + EPS)
        factor = inner / features * (inverse * inverse * inverse)
        for block in range(blocks):
            part = slice(block * per, (block + 1) * per)
            inverse_here = jnp.broadcast_to(inverse[:, part], (LANES, per)).T
            factor_here = jnp.broadcast_to(factor[:, part], (LANES, per)).T
            for half in range(2):
                cols = slice(half * width, (half + 1) * width)
                scaled = stream_ref[block, 1, :, cols].astype(jnp.float32) * gain_ref[:, cols]
                delta = scaled * inverse_here - hidden_ref[part, cols] * factor_here
                delta_ref[cols, part] = delta.T.astype(jnp.bfloat16)

    grad = jnp.dot(delta_ref[...], rows_ref[...], preferred_element_type=jnp.float32) * inv_scale
    low = grad[:width].T
    high = grad[width:].T
    first = minor_ref[0] == 0
    mine_ref[...] = jnp.where(first, low, high)
    theirs_ref[...] = jnp.where(first, high, low).astype(jnp.bfloat16)


def backward(minor, rows, hidden, stream, gain, sums, inv_scale, features):
    tokens, depth = rows.shape
    block = hidden.shape[1]
    width = block // 2
    step = 256
    return pl.pallas_call(
        functools.partial(backward_kernel, inv_scale, features),
        grid_spec=pltpu.PrefetchScalarGridSpec(
            num_scalar_prefetch=1,
            grid=(depth // step,),
            in_specs=[
                pl.BlockSpec((tokens, step), lambda i, m: (0, i)),
                pl.BlockSpec(hidden.shape, lambda i, m: (0, 0)),
                pl.BlockSpec(stream.shape, lambda i, m: (0, 0, 0, 0)),
                pl.BlockSpec((1, block), lambda i, m: (0, 0)),
                pl.BlockSpec(sums.shape, lambda i, m: (0, 0)),
            ],
            out_specs=[
                pl.BlockSpec((step, width), lambda i, m: (i, 0)),
                pl.BlockSpec((step, width), lambda i, m: (i, 0)),
            ],
            scratch_shapes=[pltpu.VMEM((block, tokens), jnp.bfloat16)],
        ),
        out_shape=[
            jax.ShapeDtypeStruct((depth, width), jnp.float32),
            jax.ShapeDtypeStruct((depth, width), jnp.bfloat16),
        ],
        compiler_params=pltpu.CompilerParams(vmem_limit_bytes=VMEM_LIMIT),
        cost_estimate=pl.CostEstimate(
            flops=2 * tokens * depth * block, bytes_accessed=8 * 1024 * 1024, transcendentals=0
        ),
        name="backward",
    )(minor, rows, hidden, stream, gain, sums)


def swap_minor(array):
    return lax.ppermute(array, "minor", [(0, 1), (1, 0)])


def sum_over_major(array):
    size = lax.axis_size("major")
    reach = 1
    while reach < size:
        array = array + lax.ppermute(array, "major", [(i, i ^ reach) for i in range(size)])
        reach *= 2
    return array


def exchange(array, sources):
    out = lax.all_to_all(array, "member", split_axis=0, concat_axis=0, tiled=True)
    return lax.all_to_all(out[sources], "member", split_axis=0, concat_axis=0, tiled=True)


def spread_features(residual, upstream):
    size = lax.axis_size("major")
    me = lax.axis_index("major")
    block = residual.shape[1] // size
    received = []
    for shift in range(size):
        start = lax.rem(me + shift, size) * block
        part = jnp.stack(
            (
                lax.dynamic_slice_in_dim(residual, start, block, axis=1),
                lax.dynamic_slice_in_dim(upstream, start, block, axis=1),
            )
        )
        if shift:
            part = lax.ppermute(part, "major", [(i, (i + shift) % size) for i in range(size)])
        received.append(part)
    return jnp.stack(received)[lax.rem(me + size - jnp.arange(size), size)]


def local(
    attention_out,
    residual,
    upstream,
    norm_gain,
    weight,
    first_moment,
    second_moment,
    sources,
    rate_index,
):
    members = lax.axis_size("member")
    minor = lax.axis_index("minor")
    depth, width = weight.shape[1:]
    rows = depth // members
    features = residual.shape[2]

    gathered = lax.all_gather(attention_out[0], "major", axis=0, tiled=True)
    weight_here = exchange(weight[0].reshape(members, rows, width), sources)
    stream = spread_features(residual[0], upstream[0])
    moments = jnp.stack(
        (first_moment[0].reshape(members, rows, width), second_moment[0].reshape(members, rows, width)),
        axis=1,
    )
    weight_here, moments = lax.optimization_barrier((weight_here, moments))
    moments = exchange(moments, sources)
    weight_here = weight_here.reshape(depth, width)
    first_here = moments[:, 0].reshape(depth, width)
    second_here = moments[:, 1].reshape(depth, width)

    gain_other = swap_minor(norm_gain[0])
    weight_other = swap_minor(weight_here)
    gain = jnp.where(
        minor == 0,
        jnp.concatenate((norm_gain[0], gain_other)),
        jnp.concatenate((gain_other, norm_gain[0])),
    ).astype(jnp.float32)[None, :]

    inv_scale = 1.0 / math.sqrt(depth)
    side = minor.astype(jnp.int32)[None]
    hidden, sums = forward(side, gathered, weight_here, weight_other, stream, gain, inv_scale)
    sums = sum_over_major(sums)
    mine, theirs = backward(side, gathered, hidden, stream, gain, sums, inv_scale, features)
    gradient = mine + swap_minor(theirs).astype(jnp.float32)

    rate_table = jnp.asarray(RATE_TABLE, dtype=jnp.float32)
    rate_value = jnp.sum(jnp.where(jnp.arange(5) == rate_index[0], rate_table, 0.0))
    weight_new, first_new, second_new = adamw_update(
        weight_here, first_here, second_here, gradient, rate_value
    )
    return (weight_new[None], first_new[None], second_new[None])


def solution(mesh):
    members, shards = mesh.devices.shape
    split = Mesh(mesh.devices.reshape(members, shards // MINOR, MINOR), ("member", "major", "minor"))
    fsdp = ("major", "minor")
    in_specs = (
        P("member", fsdp, None),
        P("member", fsdp, None),
        P("member", fsdp, None),
        P("member", fsdp),
        P("member", None, fsdp),
        P("member", None, fsdp),
        P("member", None, fsdp),
        P(),
        P("member"),
    )
    out_specs = (P("member", None, fsdp),) * 3
    return jax.shard_map(local, mesh=split, in_specs=in_specs, out_specs=out_specs, check_vma=False)
```

```python
import functools
import math

import jax
import jax.numpy as jnp
from jax import lax
from jax.experimental import pallas as pl
from jax.experimental.pallas import tpu as pltpu
from jax.sharding import Mesh
from jax.sharding import PartitionSpec as P

EPS = 1e-06
ADAM_EPS = 1e-08
BETA_ONE = 0.9
BETA_TWO = 0.95
DECAY = 0.1
bias_one = 1.0 - 0.9**10
bias_two = 1.0 - 0.95**10
RATE_TABLE = (0.02, 0.032, 0.05, 0.08, 0.125)
MINOR = 2
LANES = 128
VMEM_LIMIT = 24 * 1024 * 1024


def adamw_update(weight_now, first_now, second_now, gradient, rate_value):
    first_sum = BETA_ONE * first_now.astype(jnp.float32) + (1.0 - BETA_ONE) * gradient
    second_sum = BETA_TWO * second_now.astype(jnp.float32) + (1.0 - BETA_TWO) * gradient * gradient
    update = first_sum / bias_one / (jnp.sqrt(second_sum / bias_two) + ADAM_EPS)
    weight_new = weight_now.astype(jnp.float32) * (1.0 - rate_value * DECAY) - rate_value * update
    return (
        weight_new.astype(jnp.bfloat16),
        first_sum.astype(jnp.bfloat16),
        second_sum.astype(jnp.bfloat16),
    )


def forward_kernel(inv_scale, minor_ref, rows_ref, own_ref, other_ref, stream_ref, gain_ref, hidden_ref, sums_ref, both_ref):
    width = own_ref.shape[1]

    @pl.when(pl.program_id(0) == 0)
    def _():
        @pl.when(minor_ref[0] == 0)
        def _():
            both_ref[:, :width] = own_ref[...]
            both_ref[:, width:] = other_ref[...]

        @pl.when(minor_ref[0] != 0)
        def _():
            both_ref[:, :width] = other_ref[...]
            both_ref[:, width:] = own_ref[...]

    linear = jnp.dot(rows_ref[...], both_ref[...], preferred_element_type=jnp.float32)
    count = rows_ref.shape[0]
    stream = stream_ref[...]
    resid = stream[:, 0].reshape(count, 2 * width).astype(jnp.float32)
    upstream = stream[:, 1].reshape(count, 2 * width).astype(jnp.float32)
    hidden = resid + linear * inv_scale
    hidden_ref[...] = hidden
    scaled = upstream * gain_ref[...]
    squares = jnp.sum(hidden * hidden, axis=1, keepdims=True)
    inner = jnp.sum(scaled * hidden, axis=1, keepdims=True)
    lane = lax.broadcasted_iota(jnp.int32, (count, LANES), 1)
    packed = jnp.where(lane == 0, squares, jnp.where(lane == 1, inner, 0.0))
    sums_ref[...] = packed.T[: sums_ref.shape[0]]


def forward(minor, rows, own, other, stream, gain, inv_scale):
    tokens, depth = rows.shape
    width = own.shape[1]
    per = stream.shape[2]
    step = 2 * per
    return pl.pallas_call(
        functools.partial(forward_kernel, inv_scale),
        grid_spec=pltpu.PrefetchScalarGridSpec(
            num_scalar_prefetch=1,
            grid=(tokens // step,),
            in_specs=[
                pl.BlockSpec((step, depth), lambda i, m: (i, 0)),
                pl.BlockSpec((depth, width), lambda i, m: (0, 0)),
                pl.BlockSpec((depth, width), lambda i, m: (0, 0)),
                pl.BlockSpec((2, 2, per, 2 * width), lambda i, m: (i, 0, 0, 0)),
                pl.BlockSpec((1, 2 * width), lambda i, m: (0, 0)),
            ],
            out_specs=[
                pl.BlockSpec((step, 2 * width), lambda i, m: (i, 0)),
                pl.BlockSpec((8, step), lambda i, m: (0, i)),
            ],
            scratch_shapes=[pltpu.VMEM((depth, 2 * width), jnp.bfloat16)],
        ),
        out_shape=[
            jax.ShapeDtypeStruct((tokens, 2 * width), jnp.float32),
            jax.ShapeDtypeStruct((8, tokens), jnp.float32),
        ],
        compiler_params=pltpu.CompilerParams(vmem_limit_bytes=VMEM_LIMIT),
        cost_estimate=pl.CostEstimate(
            flops=4 * tokens * depth * width, bytes_accessed=7 * 1024 * 1024, transcendentals=0
        ),
        name="forward",
    )(minor, rows, own, other, stream, gain)


def backward_kernel(inv_scale, features, minor_ref, rows_ref, hidden_ref, stream_ref, gain_ref, sums_ref, mine_ref, theirs_ref, delta_ref):
    width = mine_ref.shape[1]
    tokens = hidden_ref.shape[0]
    blocks, _, per, _ = stream_ref.shape

    @pl.when(pl.program_id(0) == 0)
    def _():
        sums = jnp.sum(sums_ref[...].reshape(-1, 8, tokens), axis=0)
        squares = sums[0:1, :]
        inner = sums[1:2, :]
        inverse = lax.rsqrt(squares / features + EPS)
        factor = inner / features * (inverse * inverse * inverse)
        for block in range(blocks):
            part = slice(block * per, (block + 1) * per)
            inverse_here = jnp.broadcast_to(inverse[:, part], (LANES, per)).T
            factor_here = jnp.broadcast_to(factor[:, part], (LANES, per)).T
            for half in range(2):
                cols = slice(half * width, (half + 1) * width)
                scaled = stream_ref[block, 1, :, cols].astype(jnp.float32) * gain_ref[:, cols]
                delta = scaled * inverse_here - hidden_ref[part, cols] * factor_here
                delta_ref[cols, part] = delta.T.astype(jnp.bfloat16)

    grad = jnp.dot(delta_ref[...], rows_ref[...], preferred_element_type=jnp.float32) * inv_scale
    low = grad[:width].T
    high = grad[width:].T
    first = minor_ref[0] == 0
    mine_ref[...] = jnp.where(first, low, high)
    theirs_ref[...] = jnp.where(first, high, low).astype(jnp.bfloat16)


def backward(minor, rows, hidden, stream, gain, sums, inv_scale, features):
    tokens, depth = rows.shape
    block = hidden.shape[1]
    width = block // 2
    step = 256
    return pl.pallas_call(
        functools.partial(backward_kernel, inv_scale, features),
        grid_spec=pltpu.PrefetchScalarGridSpec(
            num_scalar_prefetch=1,
            grid=(depth // step,),
            in_specs=[
                pl.BlockSpec((tokens, step), lambda i, m: (0, i)),
                pl.BlockSpec(hidden.shape, lambda i, m: (0, 0)),
                pl.BlockSpec(stream.shape, lambda i, m: (0, 0, 0, 0)),
                pl.BlockSpec((1, block), lambda i, m: (0, 0)),
                pl.BlockSpec(sums.shape, lambda i, m: (0, 0)),
            ],
            out_specs=[
                pl.BlockSpec((step, width), lambda i, m: (i, 0)),
                pl.BlockSpec((step, width), lambda i, m: (i, 0)),
            ],
            scratch_shapes=[pltpu.VMEM((block, tokens), jnp.bfloat16)],
        ),
        out_shape=[
            jax.ShapeDtypeStruct((depth, width), jnp.float32),
            jax.ShapeDtypeStruct((depth, width), jnp.bfloat16),
        ],
        compiler_params=pltpu.CompilerParams(vmem_limit_bytes=VMEM_LIMIT),
        cost_estimate=pl.CostEstimate(
            flops=2 * tokens * depth * block, bytes_accessed=8 * 1024 * 1024, transcendentals=0
        ),
        name="backward",
    )(minor, rows, hidden, stream, gain, sums)


def swap_minor(array):
    return lax.ppermute(array, "minor", [(0, 1), (1, 0)])


def spread_members(array):
    return lax.all_to_all(array, "member", split_axis=0, concat_axis=0, tiled=True)


def spread_features(residual, upstream):
    size = lax.axis_size("major")
    me = lax.axis_index("major")
    block = residual.shape[1] // size
    received = []
    for shift in range(size):
        start = lax.rem(me + shift, size) * block
        part = jnp.stack(
            (
                lax.dynamic_slice_in_dim(residual, start, block, axis=1),
                lax.dynamic_slice_in_dim(upstream, start, block, axis=1),
            )
        )
        if shift:
            part = lax.ppermute(part, "major", [(i, (i + shift) % size) for i in range(size)])
        received.append(part)
    return received


def local(
    attention_out,
    residual,
    upstream,
    norm_gain,
    weight,
    first_moment,
    second_moment,
    sources,
    rate_index,
):
    members = lax.axis_size("member")
    minor = lax.axis_index("minor")
    depth, width = weight.shape[1:]
    rows = depth // members
    features = residual.shape[2]

    gathered = lax.all_gather(attention_out[0], "major", axis=0, tiled=True)
    parts = spread_features(residual[0], upstream[0])
    gain_other = swap_minor(norm_gain[0])
    picked = spread_members(weight[0].reshape(members, rows, width))[sources]
    picked, gain_other, parts[1], parts[2], parts[7] = lax.optimization_barrier(
        (picked, gain_other, parts[1], parts[2], parts[7])
    )
    weight_here = spread_members(picked)
    moments = jnp.stack(
        (first_moment[0].reshape(members, rows, width), second_moment[0].reshape(members, rows, width)),
        axis=1,
    )
    weight_here, moments, *parts = lax.optimization_barrier((weight_here, moments, *parts))
    weight_here = weight_here.reshape(depth, width)
    weight_other = swap_minor(weight_here)
    moments = spread_members(spread_members(moments)[sources])
    first_here = moments[:, 0].reshape(depth, width)
    second_here = moments[:, 1].reshape(depth, width)
    size = len(parts)
    stream = jnp.stack(parts)[lax.rem(lax.axis_index("major") + size - jnp.arange(size), size)]

    gain = jnp.where(
        minor == 0,
        jnp.concatenate((norm_gain[0], gain_other)),
        jnp.concatenate((gain_other, norm_gain[0])),
    ).astype(jnp.float32)[None, :]

    inv_scale = 1.0 / math.sqrt(depth)
    side = minor.astype(jnp.int32)[None]
    hidden, sums = forward(side, gathered, weight_here, weight_other, stream, gain, inv_scale)
    sums = lax.all_gather(sums, "major", axis=0, tiled=True)
    mine, theirs = backward(side, gathered, hidden, stream, gain, sums, inv_scale, features)
    gradient = mine + swap_minor(theirs).astype(jnp.float32)

    rate_table = jnp.asarray(RATE_TABLE, dtype=jnp.float32)
    rate_value = jnp.sum(jnp.where(jnp.arange(5) == rate_index[0], rate_table, 0.0))
    weight_new, first_new, second_new = adamw_update(
        weight_here, first_here, second_here, gradient, rate_value
    )
    return (weight_new[None], first_new[None], second_new[None])


def solution(mesh):
    members, shards = mesh.devices.shape
    split = Mesh(mesh.devices.reshape(members, shards // MINOR, MINOR), ("member", "major", "minor"))
    fsdp = ("major", "minor")
    in_specs = (
        P("member", fsdp, None),
        P("member", fsdp, None),
        P("member", fsdp, None),
        P("member", fsdp),
        P("member", None, fsdp),
        P("member", None, fsdp),
        P("member", None, fsdp),
        P(),
        P("member"),
    )
    out_specs = (P("member", None, fsdp),) * 3
    return jax.shard_map(local, mesh=split, in_specs=in_specs, out_specs=out_specs, check_vma=False)
```

```python
import functools
import math

import jax
import jax.numpy as jnp
from jax import lax
from jax.experimental import pallas as pl
from jax.experimental.pallas import tpu as pltpu
from jax.sharding import Mesh
from jax.sharding import PartitionSpec as P

EPS = 1e-06
ADAM_EPS = 1e-08
BETA_ONE = 0.9
BETA_TWO = 0.95
DECAY = 0.1
bias_one = 1.0 - 0.9**10
bias_two = 1.0 - 0.95**10
RATE_TABLE = (0.02, 0.032, 0.05, 0.08, 0.125)
MINOR = 2
LANES = 128
VMEM_LIMIT = 24 * 1024 * 1024


def adamw_kernel(rate_ref, weight_ref, moments_ref, mine_ref, theirs_ref, weight_out, first_out, second_out):
    rate = jnp.float32(0.0)
    for slot, value in enumerate(RATE_TABLE):
        rate = jnp.where(rate_ref[0] == slot, jnp.float32(value), rate)
    shape = weight_ref.shape
    gradient = mine_ref[...] + theirs_ref[...].astype(jnp.float32)
    weight_now = weight_ref[...].astype(jnp.float32)
    first_now = moments_ref[:, 0].reshape(shape).astype(jnp.float32)
    second_now = moments_ref[:, 1].reshape(shape).astype(jnp.float32)
    first_sum = BETA_ONE * first_now + (1.0 - BETA_ONE) * gradient
    second_sum = BETA_TWO * second_now + (1.0 - BETA_TWO) * gradient * gradient
    update = first_sum / bias_one / (jnp.sqrt(second_sum / bias_two) + ADAM_EPS)
    weight_new = weight_now * (1.0 - rate * DECAY) - rate * update
    weight_out[0] = weight_new.astype(jnp.bfloat16)
    first_out[0] = first_sum.astype(jnp.bfloat16)
    second_out[0] = second_sum.astype(jnp.bfloat16)


def adamw(rate_index, weight, moments, mine, theirs):
    depth, width = weight.shape
    members, kinds, rows = moments.shape[:3]
    pieces = 4
    step = pieces * rows
    flat = pl.BlockSpec((step, width), lambda i, r: (i, 0))
    out = pl.BlockSpec((1, step, width), lambda i, r: (0, i, 0))
    return pl.pallas_call(
        adamw_kernel,
        grid_spec=pltpu.PrefetchScalarGridSpec(
            num_scalar_prefetch=1,
            grid=(members // pieces,),
            in_specs=[
                flat,
                pl.BlockSpec((pieces, kinds, rows, width), lambda i, r: (i, 0, 0, 0)),
                flat,
                flat,
            ],
            out_specs=[out, out, out],
        ),
        out_shape=[jax.ShapeDtypeStruct((1, depth, width), jnp.bfloat16)] * 3,
        compiler_params=pltpu.CompilerParams(vmem_limit_bytes=VMEM_LIMIT),
        cost_estimate=pl.CostEstimate(
            flops=20 * depth * width, bytes_accessed=18 * depth * width, transcendentals=depth * width
        ),
        name="adamw",
    )(rate_index, weight, moments, mine, theirs)


def forward_kernel(inv_scale, minor_ref, rows_ref, own_ref, other_ref, stream_ref, gain_ref, hidden_ref, sums_ref, both_ref):
    width = own_ref.shape[1]

    @pl.when(pl.program_id(0) == 0)
    def _():
        @pl.when(minor_ref[0] == 0)
        def _():
            both_ref[:, :width] = own_ref[...]
            both_ref[:, width:] = other_ref[...]

        @pl.when(minor_ref[0] != 0)
        def _():
            both_ref[:, :width] = other_ref[...]
            both_ref[:, width:] = own_ref[...]

    linear = jnp.dot(rows_ref[...], both_ref[...], preferred_element_type=jnp.float32)
    count = rows_ref.shape[0]
    stream = stream_ref[...]
    resid = stream[:, 0].reshape(count, 2 * width).astype(jnp.float32)
    upstream = stream[:, 1].reshape(count, 2 * width).astype(jnp.float32)
    hidden = resid + linear * inv_scale
    hidden_ref[...] = hidden
    scaled = upstream * gain_ref[...]
    squares = jnp.sum(hidden * hidden, axis=1, keepdims=True)
    inner = jnp.sum(scaled * hidden, axis=1, keepdims=True)
    lane = lax.broadcasted_iota(jnp.int32, (count, LANES), 1)
    packed = jnp.where(lane == 0, squares, jnp.where(lane == 1, inner, 0.0))
    sums_ref[...] = packed.T[: sums_ref.shape[0]]


def forward(minor, rows, own, other, stream, gain, inv_scale):
    tokens, depth = rows.shape
    width = own.shape[1]
    per = stream.shape[2]
    step = 2 * per
    return pl.pallas_call(
        functools.partial(forward_kernel, inv_scale),
        grid_spec=pltpu.PrefetchScalarGridSpec(
            num_scalar_prefetch=1,
            grid=(tokens // step,),
            in_specs=[
                pl.BlockSpec((step, depth), lambda i, m: (i, 0)),
                pl.BlockSpec((depth, width), lambda i, m: (0, 0)),
                pl.BlockSpec((depth, width), lambda i, m: (0, 0)),
                pl.BlockSpec((2, 2, per, 2 * width), lambda i, m: (i, 0, 0, 0)),
                pl.BlockSpec((1, 2 * width), lambda i, m: (0, 0)),
            ],
            out_specs=[
                pl.BlockSpec((step, 2 * width), lambda i, m: (i, 0)),
                pl.BlockSpec((8, step), lambda i, m: (0, i)),
            ],
            scratch_shapes=[pltpu.VMEM((depth, 2 * width), jnp.bfloat16)],
        ),
        out_shape=[
            jax.ShapeDtypeStruct((tokens, 2 * width), jnp.float32),
            jax.ShapeDtypeStruct((8, tokens), jnp.float32),
        ],
        compiler_params=pltpu.CompilerParams(vmem_limit_bytes=VMEM_LIMIT),
        cost_estimate=pl.CostEstimate(
            flops=4 * tokens * depth * width, bytes_accessed=7 * 1024 * 1024, transcendentals=0
        ),
        name="forward",
    )(minor, rows, own, other, stream, gain)


def backward_kernel(inv_scale, features, minor_ref, rows_ref, hidden_ref, stream_ref, gain_ref, sums_ref, mine_ref, theirs_ref, delta_ref):
    width = mine_ref.shape[1]
    tokens = hidden_ref.shape[0]
    blocks, _, per, _ = stream_ref.shape

    @pl.when(pl.program_id(0) == 0)
    def _():
        squares = sums_ref[0:1, :]
        inner = sums_ref[1:2, :]
        inverse = lax.rsqrt(squares / features + EPS)
        factor = inner / features * (inverse * inverse * inverse)
        for block in range(blocks):
            part = slice(block * per, (block + 1) * per)
            inverse_here = jnp.broadcast_to(inverse[:, part], (LANES, per)).T
            factor_here = jnp.broadcast_to(factor[:, part], (LANES, per)).T
            for half in range(2):
                cols = slice(half * width, (half + 1) * width)
                scaled = stream_ref[block, 1, :, cols].astype(jnp.float32) * gain_ref[:, cols]
                delta = scaled * inverse_here - hidden_ref[part, cols] * factor_here
                delta_ref[cols, part] = delta.T.astype(jnp.bfloat16)

    grad = jnp.dot(delta_ref[...], rows_ref[...], preferred_element_type=jnp.float32) * inv_scale
    low = grad[:width].T
    high = grad[width:].T
    first = minor_ref[0] == 0
    mine_ref[...] = jnp.where(first, low, high)
    theirs_ref[...] = jnp.where(first, high, low).astype(jnp.bfloat16)


def backward(minor, rows, hidden, stream, gain, sums, inv_scale, features):
    tokens, depth = rows.shape
    block = hidden.shape[1]
    width = block // 2
    step = 256
    return pl.pallas_call(
        functools.partial(backward_kernel, inv_scale, features),
        grid_spec=pltpu.PrefetchScalarGridSpec(
            num_scalar_prefetch=1,
            grid=(depth // step,),
            in_specs=[
                pl.BlockSpec((tokens, step), lambda i, m: (0, i)),
                pl.BlockSpec(hidden.shape, lambda i, m: (0, 0)),
                pl.BlockSpec(stream.shape, lambda i, m: (0, 0, 0, 0)),
                pl.BlockSpec((1, block), lambda i, m: (0, 0)),
                pl.BlockSpec(sums.shape, lambda i, m: (0, 0)),
            ],
            out_specs=[
                pl.BlockSpec((step, width), lambda i, m: (i, 0)),
                pl.BlockSpec((step, width), lambda i, m: (i, 0)),
            ],
            scratch_shapes=[pltpu.VMEM((block, tokens), jnp.bfloat16)],
        ),
        out_shape=[
            jax.ShapeDtypeStruct((depth, width), jnp.float32),
            jax.ShapeDtypeStruct((depth, width), jnp.bfloat16),
        ],
        compiler_params=pltpu.CompilerParams(vmem_limit_bytes=VMEM_LIMIT),
        cost_estimate=pl.CostEstimate(
            flops=2 * tokens * depth * block, bytes_accessed=8 * 1024 * 1024, transcendentals=0
        ),
        name="backward",
    )(minor, rows, hidden, stream, gain, sums)


def swap_minor(array):
    return lax.ppermute(array, "minor", [(0, 1), (1, 0)])


def sum_over_major(array):
    size = lax.axis_size("major")
    reach = 1
    while reach < size:
        array = array + lax.ppermute(array, "major", [(i, i ^ reach) for i in range(size)])
        reach *= 2
    return array


def spread_members(array):
    return lax.all_to_all(array, "member", split_axis=0, concat_axis=0, tiled=True)


def spread_features(residual, upstream):
    size = lax.axis_size("major")
    me = lax.axis_index("major")
    block = residual.shape[1] // size
    received = []
    for shift in range(size):
        start = lax.rem(me + shift, size) * block
        part = jnp.stack(
            (
                lax.dynamic_slice_in_dim(residual, start, block, axis=1),
                lax.dynamic_slice_in_dim(upstream, start, block, axis=1),
            )
        )
        if shift:
            part = lax.ppermute(part, "major", [(i, (i + shift) % size) for i in range(size)])
        received.append(part)
    return received


def local(
    attention_out,
    residual,
    upstream,
    norm_gain,
    weight,
    first_moment,
    second_moment,
    sources,
    rate_index,
):
    members = lax.axis_size("member")
    minor = lax.axis_index("minor")
    depth, width = weight.shape[1:]
    rows = depth // members
    features = residual.shape[2]

    gathered = lax.all_gather(attention_out[0], "major", axis=0, tiled=True)
    parts = spread_features(residual[0], upstream[0])
    gain_other = swap_minor(norm_gain[0])
    picked = spread_members(weight[0].reshape(members, rows, width))[sources]
    picked, gain_other, parts[1] = lax.optimization_barrier((picked, gain_other, parts[1]))
    weight_here = spread_members(picked)
    moments = jnp.stack(
        (first_moment[0].reshape(members, rows, width), second_moment[0].reshape(members, rows, width)),
        axis=1,
    )
    weight_here, moments, parts[2], parts[6], parts[7] = lax.optimization_barrier(
        (weight_here, moments, parts[2], parts[6], parts[7])
    )
    weight_here = weight_here.reshape(depth, width)
    weight_other = swap_minor(weight_here)
    moments = spread_members(moments)
    size = len(parts)
    stream = jnp.stack(parts)[lax.rem(lax.axis_index("major") + size - jnp.arange(size), size)]

    gain = jnp.where(
        minor == 0,
        jnp.concatenate((norm_gain[0], gain_other)),
        jnp.concatenate((gain_other, norm_gain[0])),
    ).astype(jnp.float32)[None, :]

    inv_scale = 1.0 / math.sqrt(depth)
    side = minor.astype(jnp.int32)[None]
    hidden, sums = forward(side, gathered, weight_here, weight_other, stream, gain, inv_scale)
    moments, sums = lax.optimization_barrier((moments, sums))
    moments = spread_members(moments[sources])
    sums = sum_over_major(sums)
    mine, theirs = backward(side, gathered, hidden, stream, gain, sums, inv_scale, features)
    return adamw(rate_index, weight_here, moments, mine, swap_minor(theirs))


def solution(mesh):
    members, shards = mesh.devices.shape
    split = Mesh(mesh.devices.reshape(members, shards // MINOR, MINOR), ("member", "major", "minor"))
    fsdp = ("major", "minor")
    in_specs = (
        P("member", fsdp, None),
        P("member", fsdp, None),
        P("member", fsdp, None),
        P("member", fsdp),
        P("member", None, fsdp),
        P("member", None, fsdp),
        P("member", None, fsdp),
        P(),
        P("member"),
    )
    out_specs = (P("member", None, fsdp),) * 3
    return jax.shard_map(local, mesh=split, in_specs=in_specs, out_specs=out_specs, check_vma=False)
```

```python
import functools
import math

import jax
import jax.numpy as jnp
from jax import lax
from jax.experimental import pallas as pl
from jax.experimental.pallas import tpu as pltpu
from jax.sharding import Mesh
from jax.sharding import PartitionSpec as P

EPS = 1e-06
ADAM_EPS = 1e-08
BETA_ONE = 0.9
BETA_TWO = 0.95
DECAY = 0.1
bias_one = 1.0 - 0.9**10
bias_two = 1.0 - 0.95**10
RATE_TABLE = (0.02, 0.032, 0.05, 0.08, 0.125)
MINOR = 2
PLANES = 4
FEW = 2
LANES = 128
VMEM_LIMIT = 24 * 1024 * 1024


def adamw_kernel(rate_ref, weight_ref, moments_ref, mine_ref, theirs_ref, weight_out, first_out, second_out):
    rate = jnp.float32(0.0)
    for slot, value in enumerate(RATE_TABLE):
        rate = jnp.where(rate_ref[0] == slot, jnp.float32(value), rate)
    shape = weight_ref.shape
    gradient = mine_ref[...] + theirs_ref[...].astype(jnp.float32)
    weight_now = weight_ref[...].astype(jnp.float32)
    first_now = moments_ref[:, 0].reshape(shape).astype(jnp.float32)
    second_now = moments_ref[:, 1].reshape(shape).astype(jnp.float32)
    first_sum = BETA_ONE * first_now + (1.0 - BETA_ONE) * gradient
    second_sum = BETA_TWO * second_now + (1.0 - BETA_TWO) * gradient * gradient
    update = first_sum / bias_one / (jnp.sqrt(second_sum / bias_two) + ADAM_EPS)
    weight_new = weight_now * (1.0 - rate * DECAY) - rate * update
    weight_out[0] = weight_new.astype(jnp.bfloat16)
    first_out[0] = first_sum.astype(jnp.bfloat16)
    second_out[0] = second_sum.astype(jnp.bfloat16)


def adamw(rate_index, weight, moments, mine, theirs):
    depth, width = weight.shape
    members, kinds, rows = moments.shape[:3]
    pieces = 1
    step = pieces * rows
    flat = pl.BlockSpec((step, width), lambda i, r: (i, 0))
    out = pl.BlockSpec((1, step, width), lambda i, r: (0, i, 0))
    return pl.pallas_call(
        adamw_kernel,
        grid_spec=pltpu.PrefetchScalarGridSpec(
            num_scalar_prefetch=1,
            grid=(members // pieces,),
            in_specs=[
                flat,
                pl.BlockSpec((pieces, kinds, rows, width), lambda i, r: (i, 0, 0, 0)),
                flat,
                flat,
            ],
            out_specs=[out, out, out],
        ),
        out_shape=[jax.ShapeDtypeStruct((1, depth, width), jnp.bfloat16)] * 3,
        compiler_params=pltpu.CompilerParams(vmem_limit_bytes=VMEM_LIMIT),
        cost_estimate=pl.CostEstimate(
            flops=20 * depth * width, bytes_accessed=18 * depth * width, transcendentals=depth * width
        ),
        name="adamw",
    )(rate_index, weight, moments, mine, theirs)


def forward_kernel(inv_scale, minor_ref, rows_ref, own_ref, other_ref, stream_ref, gain_ref, hidden_ref, sums_ref, both_ref):
    width = own_ref.shape[1]

    @pl.when(pl.program_id(0) == 0)
    def _():
        @pl.when(minor_ref[0] == 0)
        def _():
            both_ref[:, :width] = own_ref[...]
            both_ref[:, width:] = other_ref[...]

        @pl.when(minor_ref[0] != 0)
        def _():
            both_ref[:, :width] = other_ref[...]
            both_ref[:, width:] = own_ref[...]

    linear = jnp.dot(rows_ref[...], both_ref[...], preferred_element_type=jnp.float32)
    count = rows_ref.shape[0]
    stream = stream_ref[...]
    resid = stream[:, 0].reshape(count, 2 * width).astype(jnp.float32)
    upstream = stream[:, 1].reshape(count, 2 * width).astype(jnp.float32)
    hidden = resid + linear * inv_scale
    hidden_ref[...] = hidden
    scaled = upstream * gain_ref[...]
    squares = jnp.sum(hidden * hidden, axis=1, keepdims=True)
    inner = jnp.sum(scaled * hidden, axis=1, keepdims=True)
    lane = lax.broadcasted_iota(jnp.int32, (count, LANES), 1)
    packed = jnp.where(lane == 0, squares, jnp.where(lane == 1, inner, 0.0))
    sums_ref[...] = packed.T[: sums_ref.shape[0]]


def forward(minor, rows, own, other, stream, gain, inv_scale):
    tokens, depth = rows.shape
    width = own.shape[1]
    per = stream.shape[2]
    step = 2 * per
    return pl.pallas_call(
        functools.partial(forward_kernel, inv_scale),
        grid_spec=pltpu.PrefetchScalarGridSpec(
            num_scalar_prefetch=1,
            grid=(tokens // step,),
            in_specs=[
                pl.BlockSpec((step, depth), lambda i, m: (i, 0)),
                pl.BlockSpec((depth, width), lambda i, m: (0, 0)),
                pl.BlockSpec((depth, width), lambda i, m: (0, 0)),
                pl.BlockSpec((2, 2, per, 2 * width), lambda i, m: (i, 0, 0, 0)),
                pl.BlockSpec((1, 2 * width), lambda i, m: (0, 0)),
            ],
            out_specs=[
                pl.BlockSpec((step, 2 * width), lambda i, m: (i, 0)),
                pl.BlockSpec((8, step), lambda i, m: (0, i)),
            ],
            scratch_shapes=[pltpu.VMEM((depth, 2 * width), jnp.bfloat16)],
        ),
        out_shape=[
            jax.ShapeDtypeStruct((tokens, 2 * width), jnp.float32),
            jax.ShapeDtypeStruct((8, tokens), jnp.float32),
        ],
        compiler_params=pltpu.CompilerParams(vmem_limit_bytes=VMEM_LIMIT),
        cost_estimate=pl.CostEstimate(
            flops=4 * tokens * depth * width, bytes_accessed=7 * 1024 * 1024, transcendentals=0
        ),
        name="forward",
    )(minor, rows, own, other, stream, gain)


def backward_kernel(inv_scale, features, minor_ref, rows_ref, hidden_ref, stream_ref, gain_ref, sums_ref, mine_ref, theirs_ref, delta_ref):
    width = mine_ref.shape[1]
    tokens = hidden_ref.shape[0]
    blocks, _, per, _ = stream_ref.shape

    @pl.when(pl.program_id(0) == 0)
    def _():
        sums = jnp.sum(sums_ref[...], axis=0)
        squares = sums[0:1, :]
        inner = sums[1:2, :]
        inverse = lax.rsqrt(squares / features + EPS)
        factor = inner / features * (inverse * inverse * inverse)
        for block in range(blocks):
            part = slice(block * per, (block + 1) * per)
            inverse_here = jnp.broadcast_to(inverse[:, part], (LANES, per)).T
            factor_here = jnp.broadcast_to(factor[:, part], (LANES, per)).T
            for half in range(2):
                cols = slice(half * width, (half + 1) * width)
                scaled = stream_ref[block, 1, :, cols].astype(jnp.float32) * gain_ref[:, cols]
                delta = scaled * inverse_here - hidden_ref[part, cols] * factor_here
                delta_ref[cols, part] = delta.T.astype(jnp.bfloat16)

    grad = jnp.dot(delta_ref[...], rows_ref[...], preferred_element_type=jnp.float32) * inv_scale
    low = grad[:width].T
    high = grad[width:].T
    first = minor_ref[0] == 0
    mine_ref[...] = jnp.where(first, low, high)
    theirs_ref[...] = jnp.where(first, high, low).astype(jnp.bfloat16)


def backward(minor, rows, hidden, stream, gain, sums, inv_scale, features):
    tokens, depth = rows.shape
    block = hidden.shape[1]
    width = block // 2
    step = 256
    return pl.pallas_call(
        functools.partial(backward_kernel, inv_scale, features),
        grid_spec=pltpu.PrefetchScalarGridSpec(
            num_scalar_prefetch=1,
            grid=(depth // step,),
            in_specs=[
                pl.BlockSpec((tokens, step), lambda i, m: (0, i)),
                pl.BlockSpec(hidden.shape, lambda i, m: (0, 0)),
                pl.BlockSpec(stream.shape, lambda i, m: (0, 0, 0, 0)),
                pl.BlockSpec((1, block), lambda i, m: (0, 0)),
                pl.BlockSpec(sums.shape, lambda i, m: (0, 0, 0)),
            ],
            out_specs=[
                pl.BlockSpec((step, width), lambda i, m: (i, 0)),
                pl.BlockSpec((step, width), lambda i, m: (i, 0)),
            ],
            scratch_shapes=[pltpu.VMEM((block, tokens), jnp.bfloat16)],
        ),
        out_shape=[
            jax.ShapeDtypeStruct((depth, width), jnp.float32),
            jax.ShapeDtypeStruct((depth, width), jnp.bfloat16),
        ],
        compiler_params=pltpu.CompilerParams(vmem_limit_bytes=VMEM_LIMIT),
        cost_estimate=pl.CostEstimate(
            flops=2 * tokens * depth * block, bytes_accessed=8 * 1024 * 1024, transcendentals=0
        ),
        name="backward",
    )(minor, rows, hidden, stream, gain, sums)


def swap_minor(array):
    return lax.ppermute(array, "minor", [(0, 1), (1, 0)])


def sums_of_all(sums):
    size = lax.axis_size("major")
    copies = jnp.broadcast_to(sums[None, :2], (size, 2, sums.shape[1]))
    return lax.all_to_all(copies, "major", split_axis=0, concat_axis=0, tiled=True)


def spread_columns(array):
    return lax.all_to_all(array, "column", split_axis=0, concat_axis=0, tiled=True)


def plan_moves(sources):
    planes = lax.axis_size("plane")
    columns = lax.axis_size("column")
    me = lax.axis_index("plane")
    member = jnp.arange(planes * columns, dtype=jnp.int32)
    here, there = member // columns, sources // columns
    offset = lax.rem(here - there + planes, planes)
    earlier = member[None, :] < member[:, None]
    same = (here[None, :] == here[:, None]) & (there[None, :] == there[:, None])
    rank = jnp.sum((earlier & same).astype(jnp.int32), axis=1)
    most = jnp.max(jnp.where(offset > 0, rank, 0))
    shifts = jnp.arange(1, planes, dtype=jnp.int32)[:, None, None]
    slots = jnp.arange(columns, dtype=jnp.int32)[None, :, None]
    leaving = (there == me)[None, None, :] & (offset[None, None, :] == shifts) & (rank[None, None, :] == slots)
    outgoing = jnp.sum(jnp.where(leaving, lax.rem(sources, columns)[None, None, :], 0), axis=2)
    mine = lambda values: lax.dynamic_slice_in_dim(values, me * columns, columns)
    return mine(lax.rem(sources, columns)), mine(offset), mine(rank), outgoing, most


def send_planes(pieces, outgoing):
    planes = lax.axis_size("plane")
    count = outgoing.shape[1]
    packed = pieces[outgoing.reshape(-1)]
    return [
        lax.ppermute(
            packed[(shift - 1) * count : shift * count],
            "plane",
            [(i, (i + shift) % planes) for i in range(planes)],
        )
        for shift in range(1, planes)
    ]


def choose(pieces, received, plan):
    column, offset, rank = plan[:3]
    count = received[0].shape[0]
    index = jnp.where(offset == 0, column, pieces.shape[0] + (offset - 1) * count + rank)
    return jnp.concatenate((pieces, *received))[index]


def cross_planes(pieces, received, plan):
    few = received[0].shape[0]

    def all_slots(pieces, received):
        rest = send_planes(pieces, plan[3][:, few:])
        whole = [jnp.concatenate(pair) for pair in zip(received, rest)]
        return choose(pieces, whole, plan)

    def few_slots(pieces, received):
        return choose(pieces, received, plan)

    return lax.cond(plan[4] >= few, all_slots, few_slots, pieces, received)


def spread_features(residual, upstream):
    size = lax.axis_size("major")
    me = lax.axis_index("major")
    block = residual.shape[1] // size
    received = []
    for shift in range(size):
        start = lax.rem(me + shift, size) * block
        part = jnp.stack(
            (
                lax.dynamic_slice_in_dim(residual, start, block, axis=1),
                lax.dynamic_slice_in_dim(upstream, start, block, axis=1),
            )
        )
        if shift:
            part = lax.ppermute(part, "major", [(i, (i + shift) % size) for i in range(size)])
        received.append(part)
    return received


def local(
    attention_out,
    residual,
    upstream,
    norm_gain,
    weight,
    first_moment,
    second_moment,
    sources,
    rate_index,
):
    columns = lax.axis_size("column")
    minor = lax.axis_index("minor")
    depth, width = weight.shape[1:]
    rows = depth // columns
    features = residual.shape[2]

    gathered = lax.all_gather(attention_out[0], "major", axis=0, tiled=True)
    plan = plan_moves(sources)
    few = plan[3][:, :FEW]
    parts = spread_features(residual[0], upstream[0])
    gain_other = swap_minor(norm_gain[0])
    weights = spread_columns(weight[0].reshape(columns, rows, width))
    moments = jnp.stack(
        (first_moment[0].reshape(columns, rows, width), second_moment[0].reshape(columns, rows, width)),
        axis=1,
    )
    weights, moments, gain_other, parts[1] = lax.optimization_barrier(
        (weights, moments, gain_other, parts[1])
    )
    weights_in = send_planes(weights, few)
    moments = spread_columns(moments)
    weights = cross_planes(weights, weights_in, plan)
    weights, moments, parts[2], parts[7] = lax.optimization_barrier(
        (weights, moments, parts[2], parts[7])
    )
    weight_here = spread_columns(weights).reshape(depth, width)
    weight_other = swap_minor(weight_here)
    moments_in = send_planes(moments, few)
    size = len(parts)
    stream = jnp.stack(parts)[lax.rem(lax.axis_index("major") + size - jnp.arange(size), size)]

    gain = jnp.where(
        minor == 0,
        jnp.concatenate((norm_gain[0], gain_other)),
        jnp.concatenate((gain_other, norm_gain[0])),
    ).astype(jnp.float32)[None, :]

    inv_scale = 1.0 / math.sqrt(depth)
    side = minor.astype(jnp.int32)[None]
    hidden, sums = forward(side, gathered, weight_here, weight_other, stream, gain, inv_scale)
    moments_in, sums = lax.optimization_barrier((moments_in, sums))
    sums = sums_of_all(sums)
    moments = cross_planes(moments, moments_in, plan)
    moments, sums = lax.optimization_barrier((moments, sums))
    moments = spread_columns(moments)
    mine, theirs = backward(side, gathered, hidden, stream, gain, sums, inv_scale, features)
    return adamw(rate_index, weight_here, moments, mine, swap_minor(theirs))


def solution(mesh):
    members, shards = mesh.devices.shape
    split = Mesh(
        mesh.devices.reshape(PLANES, members // PLANES, shards // MINOR, MINOR),
        ("plane", "column", "major", "minor"),
    )
    member, fsdp = ("plane", "column"), ("major", "minor")
    in_specs = (
        P(member, fsdp, None),
        P(member, fsdp, None),
        P(member, fsdp, None),
        P(member, fsdp),
        P(member, None, fsdp),
        P(member, None, fsdp),
        P(member, None, fsdp),
        P(),
        P(member),
    )
    out_specs = (P(member, None, fsdp),) * 3
    return jax.shard_map(local, mesh=split, in_specs=in_specs, out_specs=out_specs, check_vma=False)
```

```python
import functools
import math

import jax
import jax.numpy as jnp
from jax import lax
from jax.experimental import pallas as pl
from jax.experimental.pallas import tpu as pltpu
from jax.sharding import Mesh
from jax.sharding import PartitionSpec as P

EPS = 1e-06
ADAM_EPS = 1e-08
BETA_ONE = 0.9
BETA_TWO = 0.95
DECAY = 0.1
bias_one = 1.0 - 0.9**10
bias_two = 1.0 - 0.95**10
RATE_TABLE = (0.02, 0.032, 0.05, 0.08, 0.125)
MINOR = 2
PLANES = 4
FEW = 2
LANES = 128
VMEM_LIMIT = 56 * 1024 * 1024
KINDS = 3
HALVES = 2


def adamw_kernel(side_ref, rate_ref, weight_ref, moments_ref, mine_ref, theirs_ref, *refs):
    weight_out, first_out, second_out = refs[-3:]
    rate = jnp.float32(0.0)
    for slot, value in enumerate(RATE_TABLE):
        rate = jnp.where(rate_ref[0] == slot, jnp.float32(value), rate)
    gradient = mine_ref[...] + theirs_ref[...].astype(jnp.float32)
    weight_now = weight_ref[0, 0].astype(jnp.float32)
    first_now = moments_ref[0, 0].astype(jnp.float32)
    second_now = moments_ref[0, 1].astype(jnp.float32)
    first_sum = BETA_ONE * first_now + (1.0 - BETA_ONE) * gradient
    second_sum = BETA_TWO * second_now + (1.0 - BETA_TWO) * gradient * gradient
    update = first_sum / bias_one / (jnp.sqrt(second_sum / bias_two) + ADAM_EPS)
    weight_new = weight_now * (1.0 - rate * DECAY) - rate * update
    weight_out[0] = weight_new.astype(jnp.bfloat16)
    first_out[0] = first_sum.astype(jnp.bfloat16)
    second_out[0] = second_sum.astype(jnp.bfloat16)


def adamw(half, side, rate_index, weight, moments, mine, theirs, earlier):
    pieces, _, rows, width = weight.shape
    steps = pieces // HALVES
    first = half * steps
    flat = pl.BlockSpec((rows, width), lambda i, m, r: (i, 0))
    out = pl.BlockSpec((1, rows, width), lambda i, m, r: (0, first + i, 0))
    count = len(earlier)
    return pl.pallas_call(
        adamw_kernel,
        grid_spec=pltpu.PrefetchScalarGridSpec(
            num_scalar_prefetch=2,
            grid=(steps,),
            in_specs=[
                pl.BlockSpec((1, 1, rows, width), lambda i, m, r: (first + i, m[0], 0, 0)),
                pl.BlockSpec((1, KINDS - 1, rows, width), lambda i, m, r: (first + i, 0, 0, 0)),
                flat,
                flat,
            ]
            + [pl.BlockSpec(memory_space=pl.ANY)] * count,
            out_specs=[out, out, out],
        ),
        out_shape=[jax.ShapeDtypeStruct((1, pieces * rows, width), jnp.bfloat16)] * KINDS,
        input_output_aliases={6 + i: i for i in range(count)},
        compiler_params=pltpu.CompilerParams(vmem_limit_bytes=VMEM_LIMIT),
        cost_estimate=pl.CostEstimate(
            flops=20 * steps * rows * width,
            bytes_accessed=18 * steps * rows * width,
            transcendentals=steps * rows * width,
        ),
        name="adamw",
    )(side, rate_index, weight, moments, mine, theirs, *earlier)


def forward_kernel(inv_scale, shifts, major_ref, near_ref, far_ref, weight_ref, gain_ref, *refs):
    parts = refs[:shifts]
    hidden_ref, sums_ref, both_ref, rows_ref = refs[shifts : shifts + 4]
    part_ref = refs[-1]
    pieces, halves, rows, width = weight_ref.shape
    step = pl.program_id(0)
    per = near_ref.shape[0]

    @pl.when(step == 0)
    def _():
        for piece in range(pieces):
            for half in range(halves):
                both_ref[piece * rows : (piece + 1) * rows, half * width : (half + 1) * width] = weight_ref[piece, half]

    for now in range(shifts // 2):
        @pl.when(step == now)
        def _():
            part_ref[0] = parts[2 * now][...]
            part_ref[1] = parts[2 * now + 1][...]

    rows_ref[:per] = near_ref[...]
    rows_ref[per:] = far_ref[...]
    linear = jnp.dot(rows_ref[...], both_ref[...], preferred_element_type=jnp.float32)
    lane = lax.broadcasted_iota(jnp.int32, (per, LANES), 1)
    for which in range(2):
        origin = lax.rem(major_ref[0] + shifts - 2 * step - which, shifts)
        place = pl.ds(pl.multiple_of(origin * per, per), per)
        hidden = part_ref[which, 0].astype(jnp.float32) + linear[which * per : (which + 1) * per] * inv_scale
        hidden_ref[place, :] = hidden
        scaled = part_ref[which, 1].astype(jnp.float32) * gain_ref[...]
        squares = jnp.sum(hidden * hidden, axis=1, keepdims=True)
        inner = jnp.sum(scaled * hidden, axis=1, keepdims=True)
        packed = jnp.where(lane == 0, squares, jnp.where(lane == 1, inner, 0.0)).T[:2]
        for target in range(shifts):
            sums_ref[target, :, place] = packed


def forward(major, rows, weight, gain, parts, inv_scale):
    tokens, depth = rows.shape
    shifts = len(parts)
    per = tokens // shifts
    block = 2 * weight.shape[3]
    near = lambda which: pl.BlockSpec((per, depth), lambda i, m: (lax.rem(m[0] + shifts - 2 * i - which, shifts), 0))
    return pl.pallas_call(
        functools.partial(forward_kernel, inv_scale, shifts),
        grid_spec=pltpu.PrefetchScalarGridSpec(
            num_scalar_prefetch=1,
            grid=(shifts // 2,),
            in_specs=[
                near(0),
                near(1),
                pl.BlockSpec(weight.shape, lambda i, m: (0, 0, 0, 0)),
                pl.BlockSpec(gain.shape, lambda i, m: (0, 0)),
            ]
            + [pl.BlockSpec(part.shape, lambda i, m: (0, 0, 0)) for part in parts],
            out_specs=[
                pl.BlockSpec((tokens, block), lambda i, m: (0, 0)),
                pl.BlockSpec((shifts, 2, tokens), lambda i, m: (0, 0, 0)),
            ],
            scratch_shapes=[
                pltpu.VMEM((depth, block), jnp.bfloat16),
                pltpu.VMEM((2 * per, depth), jnp.bfloat16),
                pltpu.VMEM((2, 2, per, block), jnp.bfloat16),
            ],
        ),
        out_shape=[
            jax.ShapeDtypeStruct((tokens, block), jnp.float32),
            jax.ShapeDtypeStruct((shifts, 2, tokens), jnp.float32),
        ],
        compiler_params=pltpu.CompilerParams(vmem_limit_bytes=VMEM_LIMIT),
        cost_estimate=pl.CostEstimate(
            flops=2 * tokens * depth * block, bytes_accessed=7 * 1024 * 1024, transcendentals=0
        ),
        name="forward",
    )(major, rows, rows, weight, gain, *parts)


def multiply(inv_scale, side_ref, delta, rows_ref, mine_ref, theirs_ref):
    width = mine_ref.shape[1]
    grad = jnp.dot(delta, rows_ref[...], preferred_element_type=jnp.float32) * inv_scale
    low = grad[:width].T
    high = grad[width:].T
    first = side_ref[0] == 0
    mine_ref[...] = jnp.where(first, low, high)
    theirs_ref[...] = jnp.where(first, high, low).astype(jnp.bfloat16)


def backward_first_kernel(inv_scale, features, shifts, side_ref, major_ref, rows_ref, hidden_ref, gain_ref, sums_ref, *refs):
    parts = refs[:shifts]
    mine_ref, theirs_ref, delta_ref = refs[shifts:]
    width = mine_ref.shape[1]
    per = hidden_ref.shape[0] // shifts

    @pl.when(pl.program_id(0) == 0)
    def _():
        for shift in range(shifts):
            origin = lax.rem(major_ref[0] + shifts - shift, shifts)
            place = pl.ds(pl.multiple_of(origin * per, per), per)
            sums = jnp.sum(sums_ref[:, :, place], axis=0)
            inverse = lax.rsqrt(sums[0:1] / features + EPS)
            factor = sums[1:2] / features * (inverse * inverse * inverse)
            inverse_here = jnp.broadcast_to(inverse, (LANES, per)).T
            factor_here = jnp.broadcast_to(factor, (LANES, per)).T
            for half in range(2):
                cols = slice(half * width, (half + 1) * width)
                scaled = parts[shift][1, :, cols].astype(jnp.float32) * gain_ref[:, cols]
                delta = scaled * inverse_here - hidden_ref[place, cols] * factor_here
                delta_ref[cols, place] = delta.T.astype(jnp.bfloat16)

    multiply(inv_scale, side_ref, delta_ref[...], rows_ref, mine_ref, theirs_ref)


def backward_next_kernel(inv_scale, side_ref, rows_ref, delta_ref, mine_ref, theirs_ref):
    multiply(inv_scale, side_ref, delta_ref[...], rows_ref, mine_ref, theirs_ref)


def backward(side, major, rows, hidden, gain, sums, parts, inv_scale, features):
    tokens, depth = rows.shape
    block = hidden.shape[1]
    width = block // 2
    step = 256
    steps = depth // step // HALVES
    params = pltpu.CompilerParams(vmem_limit_bytes=VMEM_LIMIT)
    cost = pl.CostEstimate(
        flops=2 * tokens * depth * block // HALVES, bytes_accessed=5 * 1024 * 1024, transcendentals=0
    )
    outs = [
        jax.ShapeDtypeStruct((depth // HALVES, width), jnp.float32),
        jax.ShapeDtypeStruct((depth // HALVES, width), jnp.bfloat16),
    ]
    whole = lambda array: pl.BlockSpec(array.shape, lambda i, *_: (0,) * array.ndim)
    delta = jax.ShapeDtypeStruct((block, tokens), jnp.bfloat16)
    out = pl.BlockSpec((step, width), lambda i, *_: (i, 0))
    *first, delta = pl.pallas_call(
        functools.partial(backward_first_kernel, inv_scale, features, len(parts)),
        grid_spec=pltpu.PrefetchScalarGridSpec(
            num_scalar_prefetch=2,
            grid=(steps,),
            in_specs=[pl.BlockSpec((tokens, step), lambda i, *_: (0, i)), whole(hidden), whole(gain), whole(sums)]
            + [whole(part) for part in parts],
            out_specs=[out, out, whole(delta)],
        ),
        out_shape=outs + [delta],
        compiler_params=params,
        cost_estimate=cost,
        name="backward_first",
    )(side, major, rows, hidden, gain, sums, *parts)
    result = [first]
    for half in range(1, HALVES):
        result.append(
            pl.pallas_call(
                functools.partial(backward_next_kernel, inv_scale),
                grid_spec=pltpu.PrefetchScalarGridSpec(
                    num_scalar_prefetch=1,
                    grid=(steps,),
                    in_specs=[
                        pl.BlockSpec((tokens, step), lambda i, *_, half=half: (0, half * steps + i)),
                        whole(delta),
                    ],
                    out_specs=[out, out],
                ),
                out_shape=outs,
                compiler_params=params,
                cost_estimate=cost,
                name="backward_next",
            )(side, rows, delta)
        )
    return result


def swap_minor(array):
    return lax.ppermute(array, "minor", [(0, 1), (1, 0)])


def sums_of_all(sums):
    return lax.all_to_all(sums, "major", split_axis=0, concat_axis=0, tiled=True)


def spread_columns(array):
    return lax.all_to_all(array, "column", split_axis=0, concat_axis=0, tiled=True)


def plan_moves(sources):
    planes = lax.axis_size("plane")
    columns = lax.axis_size("column")
    me = lax.axis_index("plane")
    member = jnp.arange(planes * columns, dtype=jnp.int32)
    here, there = member // columns, sources // columns
    offset = lax.rem(here - there + planes, planes)
    earlier = member[None, :] < member[:, None]
    same = (here[None, :] == here[:, None]) & (there[None, :] == there[:, None])
    rank = jnp.sum((earlier & same).astype(jnp.int32), axis=1)
    most = jnp.max(jnp.where(offset > 0, rank, 0))
    shifts = jnp.arange(1, planes, dtype=jnp.int32)[:, None, None]
    slots = jnp.arange(columns, dtype=jnp.int32)[None, :, None]
    leaving = (there == me)[None, None, :] & (offset[None, None, :] == shifts) & (rank[None, None, :] == slots)
    outgoing = jnp.sum(jnp.where(leaving, lax.rem(sources, columns)[None, None, :], 0), axis=2)
    mine = lambda values: lax.dynamic_slice_in_dim(values, me * columns, columns)
    return mine(lax.rem(sources, columns)), mine(offset), mine(rank), outgoing, most


def send_planes(pieces, outgoing, low, high):
    planes = lax.axis_size("plane")
    kinds = jnp.arange(low, high, dtype=jnp.int32)
    index = (outgoing[:, :, None] * KINDS + kinds).reshape(planes - 1, -1)
    return [
        lax.ppermute(pieces[index[shift - 1]], "plane", [(i, (i + shift) % planes) for i in range(planes)])
        for shift in range(1, planes)
    ]


def choose_kernel(low, kinds, copies, column_ref, offset_ref, rank_ref, pieces_ref, *refs):
    received, out_ref, sems = refs[:-2], refs[-2], refs[-1]
    columns = out_ref.shape[0]
    slot = lambda place, copy: out_ref.at[place, copy] if copies else out_ref.at[place]
    for place in range(columns):
        column, offset, rank = column_ref[place], offset_ref[place], rank_ref[place]
        sources = [pieces_ref.at[pl.ds(column * KINDS + low, kinds)]]
        sources += [ref.at[pl.ds(rank * kinds, kinds)] for ref in received]
        for number, source in enumerate(sources):
            @pl.when(offset == number)
            def _():
                for copy in range(max(copies, 1)):
                    pltpu.make_async_copy(source, slot(place, copy), sems.at[place, copy]).start()

    for place in range(columns):
        for copy in range(max(copies, 1)):
            pltpu.make_async_copy(pieces_ref.at[pl.ds(0, kinds)], slot(place, copy), sems.at[place, copy]).wait()


def choose(pieces, received, plan, low, high, copies):
    column, offset, rank = plan[:3]
    columns = column.shape[0]
    kinds = high - low
    lead = (columns, copies) if copies else (columns,)
    limit = received[0].shape[0] // kinds - 1
    rank = jnp.where(offset == 0, 0, jnp.minimum(rank, limit))
    anywhere = pl.BlockSpec(memory_space=pl.ANY)
    return pl.pallas_call(
        functools.partial(choose_kernel, low, kinds, copies),
        grid_spec=pltpu.PrefetchScalarGridSpec(
            num_scalar_prefetch=3,
            grid=(1,),
            in_specs=[anywhere] * (1 + len(received)),
            out_specs=anywhere,
            scratch_shapes=[pltpu.SemaphoreType.DMA((columns, max(copies, 1)))],
        ),
        out_shape=jax.ShapeDtypeStruct(lead + (kinds,) + pieces.shape[1:], pieces.dtype),
        compiler_params=pltpu.CompilerParams(vmem_limit_bytes=VMEM_LIMIT),
        name="choose",
    )(column, offset, rank, pieces, *received)


def cross_planes(pieces, received, plan, low, high, copies):
    def all_slots(pieces, received):
        rest = send_planes(pieces, plan[3][:, FEW:], low, high)
        whole = [jnp.concatenate(pair) for pair in zip(received, rest)]
        return choose(pieces, whole, plan, low, high, copies)

    def few_slots(pieces, received):
        return choose(pieces, received, plan, low, high, copies)

    return lax.cond(plan[4] >= FEW, all_slots, few_slots, pieces, received)


def spread_features(residual, upstream):
    size = lax.axis_size("major")
    me = lax.axis_index("major")
    block = residual.shape[1] // size
    received = []
    for shift in range(size):
        start = lax.rem(me + shift, size) * block
        part = jnp.stack(
            (
                lax.dynamic_slice_in_dim(residual, start, block, axis=1),
                lax.dynamic_slice_in_dim(upstream, start, block, axis=1),
            )
        )
        if shift:
            part = lax.ppermute(part, "major", [(i, (i + shift) % size) for i in range(size)])
        received.append(part)
    return received


def local(
    attention_out,
    residual,
    upstream,
    norm_gain,
    weight,
    first_moment,
    second_moment,
    sources,
    rate_index,
):
    columns = lax.axis_size("column")
    minor = lax.axis_index("minor")
    depth, width = weight.shape[1:]
    rows = depth // columns
    features = residual.shape[2]

    gathered = lax.all_gather(attention_out[0], "major", axis=0, tiled=True)
    plan = plan_moves(sources)
    few = plan[3][:, :FEW]
    state = jnp.stack(
        [array[0].reshape(columns, rows, width) for array in (weight, first_moment, second_moment)], axis=1
    )
    state = spread_columns(state).reshape(columns * KINDS, rows, width)
    parts = spread_features(residual[0], upstream[0])
    gain_other = swap_minor(norm_gain[0])
    state, gain_other, parts[1], parts[7] = lax.optimization_barrier((state, gain_other, parts[1], parts[7]))
    weights_in = send_planes(state, few, 0, 1)
    weights = cross_planes(state, weights_in, plan, 0, 1, MINOR)
    weights, state, parts[2], parts[6] = lax.optimization_barrier((weights, state, parts[2], parts[6]))
    weights = lax.all_to_all(
        weights.reshape(columns * MINOR, rows, width), ("column", "minor"), split_axis=0, concat_axis=0, tiled=True
    ).reshape(columns, MINOR, rows, width)
    moments_in = send_planes(state, few, 1, KINDS)

    gain = jnp.where(
        minor == 0,
        jnp.concatenate((norm_gain[0], gain_other)),
        jnp.concatenate((gain_other, norm_gain[0])),
    ).astype(jnp.float32)[None, :]

    inv_scale = 1.0 / math.sqrt(depth)
    side = minor.astype(jnp.int32)[None]
    major = lax.axis_index("major").astype(jnp.int32)[None]
    hidden, sums = forward(major, gathered, weights, gain, parts, inv_scale)
    moments_in, sums = lax.optimization_barrier((moments_in, sums))
    sums = sums_of_all(sums)
    moments = cross_planes(state, moments_in, plan, 1, KINDS, 0)
    moments, sums = lax.optimization_barrier((moments, sums))
    moments = spread_columns(moments)
    halves = backward(side, major, gathered, hidden, gain, sums, parts, inv_scale, features)
    result = []
    for half, (mine, theirs) in enumerate(halves):
        result = adamw(half, side, rate_index, weights, moments, mine, swap_minor(theirs), result)
    return tuple(result)


def solution(mesh):
    members, shards = mesh.devices.shape
    split = Mesh(
        mesh.devices.reshape(PLANES, members // PLANES, shards // MINOR, MINOR),
        ("plane", "column", "major", "minor"),
    )
    member, fsdp = ("plane", "column"), ("major", "minor")
    in_specs = (
        P(member, fsdp, None),
        P(member, fsdp, None),
        P(member, fsdp, None),
        P(member, fsdp),
        P(member, None, fsdp),
        P(member, None, fsdp),
        P(member, None, fsdp),
        P(),
        P(member),
    )
    out_specs = (P(member, None, fsdp),) * 3
    return jax.shard_map(local, mesh=split, in_specs=in_specs, out_specs=out_specs, check_vma=False)
```

```python
import functools
import math

import jax
import jax.numpy as jnp
from jax import lax
from jax.experimental import pallas as pl
from jax.experimental.pallas import tpu as pltpu
from jax.sharding import Mesh
from jax.sharding import PartitionSpec as P

EPS = 1e-06
ADAM_EPS = 1e-08
BETA_ONE = 0.9
BETA_TWO = 0.95
DECAY = 0.1
bias_one = 1.0 - 0.9**10
bias_two = 1.0 - 0.95**10
RATE_TABLE = (0.02, 0.032, 0.05, 0.08, 0.125)
MINOR = 2
PLANES = 4
FEW = 2
LANES = 128
VMEM_LIMIT = 24 * 1024 * 1024
FORWARD_LIMIT = 48 * 1024 * 1024
KINDS = 3
HALVES = 2


def adamw_kernel(side_ref, rate_ref, weight_ref, moments_ref, mine_ref, theirs_ref, *refs):
    weight_out, first_out, second_out = refs[-3:]
    rate = jnp.float32(0.0)
    for slot, value in enumerate(RATE_TABLE):
        rate = jnp.where(rate_ref[0] == slot, jnp.float32(value), rate)
    gradient = mine_ref[...] + theirs_ref[...].astype(jnp.float32)
    weight_now = weight_ref[0, 0].astype(jnp.float32)
    first_now = moments_ref[0, 0].astype(jnp.float32)
    second_now = moments_ref[0, 1].astype(jnp.float32)
    first_sum = BETA_ONE * first_now + (1.0 - BETA_ONE) * gradient
    second_sum = BETA_TWO * second_now + (1.0 - BETA_TWO) * gradient * gradient
    update = first_sum / bias_one / (jnp.sqrt(second_sum / bias_two) + ADAM_EPS)
    weight_new = weight_now * (1.0 - rate * DECAY) - rate * update
    weight_out[0] = weight_new.astype(jnp.bfloat16)
    first_out[0] = first_sum.astype(jnp.bfloat16)
    second_out[0] = second_sum.astype(jnp.bfloat16)


def adamw(half, side, rate_index, weight, moments, mine, theirs, earlier):
    pieces, _, rows, width = weight.shape
    steps = pieces // HALVES
    first = half * steps
    flat = pl.BlockSpec((rows, width), lambda i, m, r: (i, 0))
    out = pl.BlockSpec((1, rows, width), lambda i, m, r: (0, first + i, 0))
    count = len(earlier)
    return pl.pallas_call(
        adamw_kernel,
        grid_spec=pltpu.PrefetchScalarGridSpec(
            num_scalar_prefetch=2,
            grid=(steps,),
            in_specs=[
                pl.BlockSpec((1, 1, rows, width), lambda i, m, r: (first + i, m[0], 0, 0)),
                pl.BlockSpec((1, KINDS - 1, rows, width), lambda i, m, r: (first + i, 0, 0, 0)),
                flat,
                flat,
            ]
            + [pl.BlockSpec(memory_space=pl.ANY)] * count,
            out_specs=[out, out, out],
        ),
        out_shape=[jax.ShapeDtypeStruct((1, pieces * rows, width), jnp.bfloat16)] * KINDS,
        input_output_aliases={6 + i: i for i in range(count)},
        compiler_params=pltpu.CompilerParams(vmem_limit_bytes=VMEM_LIMIT),
        cost_estimate=pl.CostEstimate(
            flops=20 * steps * rows * width,
            bytes_accessed=18 * steps * rows * width,
            transcendentals=steps * rows * width,
        ),
        name="adamw",
    )(side, rate_index, weight, moments, mine, theirs, *earlier)


def forward_kernel(inv_scale, shifts, major_ref, near_ref, far_ref, weight_ref, gain_ref, *refs):
    parts = refs[:shifts]
    hidden_ref, sums_ref, both_ref, rows_ref = refs[shifts : shifts + 4]
    part_ref = refs[-1]
    pieces, halves, rows, width = weight_ref.shape
    step = pl.program_id(0)
    per = near_ref.shape[0]

    @pl.when(step == 0)
    def _():
        for piece in range(pieces):
            for half in range(halves):
                both_ref[piece * rows : (piece + 1) * rows, half * width : (half + 1) * width] = weight_ref[piece, half]

    for now in range(shifts // 2):
        @pl.when(step == now)
        def _():
            part_ref[0] = parts[2 * now][...]
            part_ref[1] = parts[2 * now + 1][...]

    rows_ref[:per] = near_ref[...]
    rows_ref[per:] = far_ref[...]
    linear = jnp.dot(rows_ref[...], both_ref[...], preferred_element_type=jnp.float32)
    lane = lax.broadcasted_iota(jnp.int32, (per, LANES), 1)
    for which in range(2):
        origin = lax.rem(major_ref[0] + shifts - 2 * step - which, shifts)
        place = pl.ds(pl.multiple_of(origin * per, per), per)
        hidden = part_ref[which, 0].astype(jnp.float32) + linear[which * per : (which + 1) * per] * inv_scale
        hidden_ref[place, :] = hidden
        scaled = part_ref[which, 1].astype(jnp.float32) * gain_ref[...]
        squares = jnp.sum(hidden * hidden, axis=1, keepdims=True)
        inner = jnp.sum(scaled * hidden, axis=1, keepdims=True)
        packed = jnp.where(lane == 0, squares, jnp.where(lane == 1, inner, 0.0)).T[:2]
        for target in range(shifts):
            sums_ref[target, :, place] = packed


def forward(major, rows, weight, gain, parts, inv_scale):
    tokens, depth = rows.shape
    shifts = len(parts)
    per = tokens // shifts
    block = 2 * weight.shape[3]
    near = lambda which: pl.BlockSpec((per, depth), lambda i, m: (lax.rem(m[0] + shifts - 2 * i - which, shifts), 0))
    return pl.pallas_call(
        functools.partial(forward_kernel, inv_scale, shifts),
        grid_spec=pltpu.PrefetchScalarGridSpec(
            num_scalar_prefetch=1,
            grid=(shifts // 2,),
            in_specs=[
                near(0),
                near(1),
                pl.BlockSpec(weight.shape, lambda i, m: (0, 0, 0, 0)),
                pl.BlockSpec(gain.shape, lambda i, m: (0, 0)),
            ]
            + [pl.BlockSpec(part.shape, lambda i, m: (0, 0, 0)) for part in parts],
            out_specs=[
                pl.BlockSpec((tokens, block), lambda i, m: (0, 0)),
                pl.BlockSpec((shifts, 2, tokens), lambda i, m: (0, 0, 0)),
            ],
            scratch_shapes=[
                pltpu.VMEM((depth, block), jnp.bfloat16),
                pltpu.VMEM((2 * per, depth), jnp.bfloat16),
                pltpu.VMEM((2, 2, per, block), jnp.bfloat16),
            ],
        ),
        out_shape=[
            jax.ShapeDtypeStruct((tokens, block), jnp.float32),
            jax.ShapeDtypeStruct((shifts, 2, tokens), jnp.float32),
        ],
        compiler_params=pltpu.CompilerParams(vmem_limit_bytes=FORWARD_LIMIT),
        cost_estimate=pl.CostEstimate(
            flops=2 * tokens * depth * block, bytes_accessed=7 * 1024 * 1024, transcendentals=0
        ),
        name="forward",
    )(major, rows, rows, weight, gain, *parts)


def multiply(inv_scale, side_ref, delta, rows_ref, mine_ref, theirs_ref):
    width = mine_ref.shape[1]
    grad = jnp.dot(delta, rows_ref[...], preferred_element_type=jnp.float32) * inv_scale
    low = grad[:width].T
    high = grad[width:].T
    first = side_ref[0] == 0
    mine_ref[...] = jnp.where(first, low, high)
    theirs_ref[...] = jnp.where(first, high, low).astype(jnp.bfloat16)


def backward_first_kernel(inv_scale, features, shifts, side_ref, major_ref, rows_ref, hidden_ref, gain_ref, sums_ref, *refs):
    parts = refs[:shifts]
    mine_ref, theirs_ref, delta_ref = refs[shifts:]
    width = mine_ref.shape[1]
    per = hidden_ref.shape[0] // shifts

    @pl.when(pl.program_id(0) == 0)
    def _():
        for shift in range(shifts):
            origin = lax.rem(major_ref[0] + shifts - shift, shifts)
            place = pl.ds(pl.multiple_of(origin * per, per), per)
            sums = jnp.sum(sums_ref[:, :, place], axis=0)
            inverse = lax.rsqrt(sums[0:1] / features + EPS)
            factor = sums[1:2] / features * (inverse * inverse * inverse)
            inverse_here = jnp.broadcast_to(inverse, (LANES, per)).T
            factor_here = jnp.broadcast_to(factor, (LANES, per)).T
            for half in range(2):
                cols = slice(half * width, (half + 1) * width)
                scaled = parts[shift][1, :, cols].astype(jnp.float32) * gain_ref[:, cols]
                delta = scaled * inverse_here - hidden_ref[place, cols] * factor_here
                delta_ref[cols, place] = delta.T.astype(jnp.bfloat16)

    multiply(inv_scale, side_ref, delta_ref[...], rows_ref, mine_ref, theirs_ref)


def backward_next_kernel(inv_scale, side_ref, rows_ref, delta_ref, mine_ref, theirs_ref):
    multiply(inv_scale, side_ref, delta_ref[...], rows_ref, mine_ref, theirs_ref)


def backward(side, major, rows, hidden, gain, sums, parts, inv_scale, features):
    tokens, depth = rows.shape
    block = hidden.shape[1]
    width = block // 2
    step = 256
    steps = depth // step // HALVES
    params = pltpu.CompilerParams(vmem_limit_bytes=VMEM_LIMIT)
    cost = pl.CostEstimate(
        flops=2 * tokens * depth * block // HALVES, bytes_accessed=5 * 1024 * 1024, transcendentals=0
    )
    outs = [
        jax.ShapeDtypeStruct((depth // HALVES, width), jnp.float32),
        jax.ShapeDtypeStruct((depth // HALVES, width), jnp.bfloat16),
    ]
    whole = lambda array: pl.BlockSpec(array.shape, lambda i, *_: (0,) * array.ndim)
    delta = jax.ShapeDtypeStruct((block, tokens), jnp.bfloat16)
    out = pl.BlockSpec((step, width), lambda i, *_: (i, 0))
    *first, delta = pl.pallas_call(
        functools.partial(backward_first_kernel, inv_scale, features, len(parts)),
        grid_spec=pltpu.PrefetchScalarGridSpec(
            num_scalar_prefetch=2,
            grid=(steps,),
            in_specs=[pl.BlockSpec((tokens, step), lambda i, *_: (0, i)), whole(hidden), whole(gain), whole(sums)]
            + [whole(part) for part in parts],
            out_specs=[out, out, whole(delta)],
        ),
        out_shape=outs + [delta],
        compiler_params=params,
        cost_estimate=cost,
        name="backward_first",
    )(side, major, rows, hidden, gain, sums, *parts)
    result = [first]
    for half in range(1, HALVES):
        result.append(
            pl.pallas_call(
                functools.partial(backward_next_kernel, inv_scale),
                grid_spec=pltpu.PrefetchScalarGridSpec(
                    num_scalar_prefetch=1,
                    grid=(steps,),
                    in_specs=[
                        pl.BlockSpec((tokens, step), lambda i, *_, half=half: (0, half * steps + i)),
                        whole(delta),
                    ],
                    out_specs=[out, out],
                ),
                out_shape=outs,
                compiler_params=params,
                cost_estimate=cost,
                name="backward_next",
            )(side, rows, delta)
        )
    return result


def swap_minor(array):
    return lax.ppermute(array, "minor", [(0, 1), (1, 0)])


def sums_of_all(sums):
    return lax.all_to_all(sums, "major", split_axis=0, concat_axis=0, tiled=True)


def spread_columns(array):
    return lax.all_to_all(array, "column", split_axis=0, concat_axis=0, tiled=True)


def plan_moves(sources):
    planes = lax.axis_size("plane")
    columns = lax.axis_size("column")
    me = lax.axis_index("plane")
    member = jnp.arange(planes * columns, dtype=jnp.int32)
    here, there = member // columns, sources // columns
    offset = lax.rem(here - there + planes, planes)
    earlier = member[None, :] < member[:, None]
    same = (here[None, :] == here[:, None]) & (there[None, :] == there[:, None])
    rank = jnp.sum((earlier & same).astype(jnp.int32), axis=1)
    most = jnp.max(jnp.where(offset > 0, rank, 0))
    targets = jnp.arange(planes, dtype=jnp.int32)[:, None, None]
    slots = jnp.arange(columns, dtype=jnp.int32)[None, :, None]
    leaving = (there == me) & (rank == slots)
    column = lax.rem(sources, columns)
    by_plane = jnp.sum(jnp.where(leaving & (here == targets), column, 0), axis=2)
    by_shift = jnp.sum(jnp.where(leaving & (offset == targets[1:]), column, 0), axis=2)
    mine = lambda values: lax.dynamic_slice_in_dim(values, me * columns, columns)
    return dict(
        column=mine(column),
        plane=mine(there),
        offset=mine(offset),
        rank=mine(rank),
        by_plane=by_plane,
        by_shift=by_shift,
        most=most,
    )


def pick(pieces, slots, low, high):
    kinds = jnp.arange(low, high, dtype=jnp.int32)
    return pieces[(slots[..., None] * KINDS + kinds).reshape(-1)]


def send_at_once(pieces, slots):
    return [lax.all_to_all(pick(pieces, slots, 0, 1), "plane", split_axis=0, concat_axis=0, tiled=True)]


def send_by_shift(pieces, slots):
    planes = lax.axis_size("plane")
    return [
        lax.ppermute(
            pick(pieces, slots[shift - 1], 1, KINDS), "plane", [(i, (i + shift) % planes) for i in range(planes)]
        )
        for shift in range(1, planes)
    ]


def choose_kernel(kinds, copies, which_ref, start_ref, *refs):
    refs, out_ref, sems = refs[:-2], refs[-2], refs[-1]
    columns = out_ref.shape[0]
    slot = lambda place, copy: out_ref.at[place, copy] if copies else out_ref.at[place]
    for place in range(columns):
        for number, ref in enumerate(refs):
            @pl.when(which_ref[place] == number)
            def _():
                for copy in range(max(copies, 1)):
                    source = ref.at[pl.ds(start_ref[place], kinds)]
                    pltpu.make_async_copy(source, slot(place, copy), sems.at[place, copy]).start()

    for place in range(columns):
        for copy in range(max(copies, 1)):
            pltpu.make_async_copy(refs[0].at[pl.ds(0, kinds)], slot(place, copy), sems.at[place, copy]).wait()


def choose(pieces, received, which, start, kinds, copies):
    columns = which.shape[0]
    lead = (columns, copies) if copies else (columns,)
    anywhere = pl.BlockSpec(memory_space=pl.ANY)
    return pl.pallas_call(
        functools.partial(choose_kernel, kinds, copies),
        grid_spec=pltpu.PrefetchScalarGridSpec(
            num_scalar_prefetch=2,
            grid=(1,),
            in_specs=[anywhere] * (1 + len(received)),
            out_specs=anywhere,
            scratch_shapes=[pltpu.SemaphoreType.DMA((columns, max(copies, 1)))],
        ),
        out_shape=jax.ShapeDtypeStruct(lead + (kinds,) + pieces.shape[1:], pieces.dtype),
        compiler_params=pltpu.CompilerParams(vmem_limit_bytes=VMEM_LIMIT),
        name="choose",
    )(which, start, pieces, *received)


def choose_weights(pieces, received, plan):
    stays = plan["offset"] == 0
    count = received[0].shape[0] // lax.axis_size("plane")
    away = plan["plane"] * count + jnp.minimum(plan["rank"], count - 1)
    start = jnp.where(stays, plan["column"] * KINDS, away)
    return choose(pieces, received, jnp.where(stays, 0, 1), start, 1, MINOR)


def choose_moments(pieces, received, plan):
    kinds = KINDS - 1
    last = received[0].shape[0] // kinds - 1
    away = jnp.minimum(plan["rank"], last) * kinds
    start = jnp.where(plan["offset"] == 0, plan["column"] * KINDS + 1, away)
    return choose(pieces, received, plan["offset"], start, kinds, 0)


def weights_across(pieces, received, plan):
    def all_slots(pieces, received):
        return choose_weights(pieces, send_at_once(pieces, plan["by_plane"]), plan)

    def few_slots(pieces, received):
        return choose_weights(pieces, received, plan)

    return lax.cond(plan["most"] >= FEW, all_slots, few_slots, pieces, received)


def moments_across(pieces, received, plan):
    def all_slots(pieces, received):
        return choose_moments(pieces, send_by_shift(pieces, plan["by_shift"]), plan)

    def few_slots(pieces, received):
        return choose_moments(pieces, received, plan)

    return lax.cond(plan["most"] >= FEW, all_slots, few_slots, pieces, received)


def spread_features(residual, upstream):
    size = lax.axis_size("major")
    me = lax.axis_index("major")
    block = residual.shape[1] // size
    received = []
    for shift in range(size):
        start = lax.rem(me + shift, size) * block
        part = jnp.stack(
            (
                lax.dynamic_slice_in_dim(residual, start, block, axis=1),
                lax.dynamic_slice_in_dim(upstream, start, block, axis=1),
            )
        )
        if shift:
            part = lax.ppermute(part, "major", [(i, (i + shift) % size) for i in range(size)])
        received.append(part)
    return received


def local(
    attention_out,
    residual,
    upstream,
    norm_gain,
    weight,
    first_moment,
    second_moment,
    sources,
    rate_index,
):
    columns = lax.axis_size("column")
    minor = lax.axis_index("minor")
    depth, width = weight.shape[1:]
    rows = depth // columns
    features = residual.shape[2]

    gathered = lax.all_gather(attention_out[0], "major", axis=0, tiled=True)
    plan = plan_moves(sources)
    state = jnp.stack(
        [array[0].reshape(columns, rows, width) for array in (weight, first_moment, second_moment)], axis=1
    )
    state, residual, upstream = lax.optimization_barrier((state, residual, upstream))
    state = spread_columns(state).reshape(columns * KINDS, rows, width)
    parts = spread_features(residual[0], upstream[0])
    gain_other = swap_minor(norm_gain[0])
    gain = jnp.where(
        minor == 0,
        jnp.concatenate((norm_gain[0], gain_other)),
        jnp.concatenate((gain_other, norm_gain[0])),
    ).astype(jnp.float32)[None, :]
    state, gain, parts[0], parts[1], parts[7] = lax.optimization_barrier(
        (state, gain, parts[0], parts[1], parts[7])
    )
    weights_in = send_at_once(state, plan["by_plane"][:, :FEW])
    weights = weights_across(state, weights_in, plan)
    weights, state, parts[2], parts[6] = lax.optimization_barrier((weights, state, parts[2], parts[6]))
    weights = lax.all_to_all(
        weights.reshape(columns * MINOR, rows, width), ("column", "minor"), split_axis=0, concat_axis=0, tiled=True
    ).reshape(columns, MINOR, rows, width)
    moments_in = send_by_shift(state, plan["by_shift"][:, :FEW])

    inv_scale = 1.0 / math.sqrt(depth)
    side = minor.astype(jnp.int32)[None]
    major = lax.axis_index("major").astype(jnp.int32)[None]
    hidden, sums = forward(major, gathered, weights, gain, parts, inv_scale)
    moments_in, sums = lax.optimization_barrier((moments_in, sums))
    sums = sums_of_all(sums)
    moments = moments_across(state, moments_in, plan)
    moments, sums = lax.optimization_barrier((moments, sums))
    moments = spread_columns(moments)
    halves = backward(side, major, gathered, hidden, gain, sums, parts, inv_scale, features)
    result = []
    for half, (mine, theirs) in enumerate(halves):
        result = adamw(half, side, rate_index, weights, moments, mine, swap_minor(theirs), result)
    return tuple(result)


def solution(mesh):
    members, shards = mesh.devices.shape
    split = Mesh(
        mesh.devices.reshape(PLANES, members // PLANES, shards // MINOR, MINOR),
        ("plane", "column", "major", "minor"),
    )
    member, fsdp = ("plane", "column"), ("major", "minor")
    in_specs = (
        P(member, fsdp, None),
        P(member, fsdp, None),
        P(member, fsdp, None),
        P(member, fsdp),
        P(member, None, fsdp),
        P(member, None, fsdp),
        P(member, None, fsdp),
        P(),
        P(member),
    )
    out_specs = (P(member, None, fsdp),) * 3
    return jax.shard_map(local, mesh=split, in_specs=in_specs, out_specs=out_specs, check_vma=False)
```

```python
import functools
import math

import jax
import jax.numpy as jnp
from jax import lax
from jax.experimental import pallas as pl
from jax.experimental.pallas import tpu as pltpu
from jax.sharding import Mesh
from jax.sharding import PartitionSpec as P

EPS = 1e-06
ADAM_EPS = 1e-08
BETA_ONE = 0.9
BETA_TWO = 0.95
DECAY = 0.1
bias_one = 1.0 - 0.9**10
bias_two = 1.0 - 0.95**10
RATE_TABLE = (0.02, 0.032, 0.05, 0.08, 0.125)
MINOR = 2
PLANES = 4
FEW = 2
LANES = 128
VMEM_LIMIT = 24 * 1024 * 1024
FORWARD_LIMIT = 48 * 1024 * 1024
KINDS = 3
HALVES = 2


def adamw_kernel(side_ref, rate_ref, weight_ref, moments_ref, mine_ref, theirs_ref, *refs):
    weight_out, first_out, second_out = refs[-3:]
    rate = jnp.float32(0.0)
    for slot, value in enumerate(RATE_TABLE):
        rate = jnp.where(rate_ref[0] == slot, jnp.float32(value), rate)
    gradient = mine_ref[...] + theirs_ref[...].astype(jnp.float32)
    weight_now = weight_ref[0, 0].astype(jnp.float32)
    first_now = moments_ref[0, 0].astype(jnp.float32)
    second_now = moments_ref[0, 1].astype(jnp.float32)
    first_sum = BETA_ONE * first_now + (1.0 - BETA_ONE) * gradient
    second_sum = BETA_TWO * second_now + (1.0 - BETA_TWO) * gradient * gradient
    update = first_sum / bias_one / (jnp.sqrt(second_sum / bias_two) + ADAM_EPS)
    weight_new = weight_now * (1.0 - rate * DECAY) - rate * update
    weight_out[0] = weight_new.astype(jnp.bfloat16)
    first_out[0] = first_sum.astype(jnp.bfloat16)
    second_out[0] = second_sum.astype(jnp.bfloat16)


def adamw(half, side, rate_index, weight, moments, mine, theirs, earlier):
    pieces, _, rows, width = weight.shape
    steps = pieces // HALVES
    first = half * steps
    flat = pl.BlockSpec((rows, width), lambda i, m, r: (i, 0))
    out = pl.BlockSpec((1, rows, width), lambda i, m, r: (0, first + i, 0))
    count = len(earlier)
    return pl.pallas_call(
        adamw_kernel,
        grid_spec=pltpu.PrefetchScalarGridSpec(
            num_scalar_prefetch=2,
            grid=(steps,),
            in_specs=[
                pl.BlockSpec((1, 1, rows, width), lambda i, m, r: (first + i, m[0], 0, 0)),
                pl.BlockSpec((1, KINDS - 1, rows, width), lambda i, m, r: (first + i, 0, 0, 0)),
                flat,
                flat,
            ]
            + [pl.BlockSpec(memory_space=pl.ANY)] * count,
            out_specs=[out, out, out],
        ),
        out_shape=[jax.ShapeDtypeStruct((1, pieces * rows, width), jnp.bfloat16)] * KINDS,
        input_output_aliases={6 + i: i for i in range(count)},
        compiler_params=pltpu.CompilerParams(vmem_limit_bytes=VMEM_LIMIT),
        cost_estimate=pl.CostEstimate(
            flops=20 * steps * rows * width,
            bytes_accessed=18 * steps * rows * width,
            transcendentals=steps * rows * width,
        ),
        name="adamw",
    )(side, rate_index, weight, moments, mine, theirs, *earlier)


def pack_kernel(residual_ref, upstream_ref, out_ref):
    out_ref[0, 0] = residual_ref[...]
    out_ref[0, 1] = upstream_ref[...]


def pack(residual, upstream, blocks):
    tokens, features = residual.shape
    block = features // blocks
    columns = pl.BlockSpec((tokens, block), lambda i: (0, i))
    return pl.pallas_call(
        pack_kernel,
        grid=(blocks,),
        in_specs=[columns, columns],
        out_specs=pl.BlockSpec((1, 2, tokens, block), lambda i: (i, 0, 0, 0)),
        out_shape=jax.ShapeDtypeStruct((blocks, 2, tokens, block), residual.dtype),
        compiler_params=pltpu.CompilerParams(vmem_limit_bytes=VMEM_LIMIT),
        name="pack",
    )(residual, upstream)


def forward_kernel(inv_scale, rows_ref, weight_ref, stream_ref, gain_ref, hidden_ref, sums_ref, both_ref):
    pieces, halves, rows, width = weight_ref.shape

    @pl.when(pl.program_id(0) == 0)
    def _():
        for piece in range(pieces):
            for half in range(halves):
                both_ref[piece * rows : (piece + 1) * rows, half * width : (half + 1) * width] = weight_ref[piece, half]

    linear = jnp.dot(rows_ref[...], both_ref[...], preferred_element_type=jnp.float32)
    count, block = linear.shape
    stream = stream_ref[...]
    resid = stream[:, 0].reshape(count, block).astype(jnp.float32)
    upstream = stream[:, 1].reshape(count, block).astype(jnp.float32)
    hidden = resid + linear * inv_scale
    hidden_ref[...] = hidden
    scaled = upstream * gain_ref[...]
    squares = jnp.sum(hidden * hidden, axis=1, keepdims=True)
    inner = jnp.sum(scaled * hidden, axis=1, keepdims=True)
    lane = lax.broadcasted_iota(jnp.int32, (count, LANES), 1)
    packed = jnp.where(lane == 0, squares, jnp.where(lane == 1, inner, 0.0)).T[:2]
    for target in range(sums_ref.shape[0]):
        sums_ref[target] = packed


def forward(rows, weight, gain, stream, inv_scale):
    tokens, depth = rows.shape
    blocks, _, per, block = stream.shape
    step = 2 * per
    return pl.pallas_call(
        functools.partial(forward_kernel, inv_scale),
        grid=(tokens // step,),
        in_specs=[
            pl.BlockSpec((step, depth), lambda i: (i, 0)),
            pl.BlockSpec(weight.shape, lambda i: (0, 0, 0, 0)),
            pl.BlockSpec((2, 2, per, block), lambda i: (i, 0, 0, 0)),
            pl.BlockSpec(gain.shape, lambda i: (0, 0)),
        ],
        out_specs=[
            pl.BlockSpec((step, block), lambda i: (i, 0)),
            pl.BlockSpec((blocks, 2, step), lambda i: (0, 0, i)),
        ],
        scratch_shapes=[pltpu.VMEM((depth, block), jnp.bfloat16)],
        out_shape=[
            jax.ShapeDtypeStruct((tokens, block), jnp.float32),
            jax.ShapeDtypeStruct((blocks, 2, tokens), jnp.float32),
        ],
        compiler_params=pltpu.CompilerParams(vmem_limit_bytes=FORWARD_LIMIT),
        cost_estimate=pl.CostEstimate(
            flops=2 * tokens * depth * block, bytes_accessed=7 * 1024 * 1024, transcendentals=0
        ),
        name="forward",
    )(rows, weight, stream, gain)


def multiply(inv_scale, side_ref, delta, rows_ref, mine_ref, theirs_ref):
    width = mine_ref.shape[1]
    grad = jnp.dot(delta, rows_ref[...], preferred_element_type=jnp.float32) * inv_scale
    low = grad[:width].T
    high = grad[width:].T
    first = side_ref[0] == 0
    mine_ref[...] = jnp.where(first, low, high)
    theirs_ref[...] = jnp.where(first, high, low).astype(jnp.bfloat16)


def backward_first_kernel(inv_scale, features, side_ref, rows_ref, hidden_ref, gain_ref, sums_ref, stream_ref, mine_ref, theirs_ref, delta_ref):
    width = mine_ref.shape[1]
    blocks, _, per, _ = stream_ref.shape

    @pl.when(pl.program_id(0) == 0)
    def _():
        sums = jnp.sum(sums_ref[...], axis=0)
        inverse = lax.rsqrt(sums[0:1] / features + EPS)
        factor = sums[1:2] / features * (inverse * inverse * inverse)
        for block in range(blocks):
            place = slice(block * per, (block + 1) * per)
            inverse_here = jnp.broadcast_to(inverse[:, place], (LANES, per)).T
            factor_here = jnp.broadcast_to(factor[:, place], (LANES, per)).T
            for half in range(2):
                cols = slice(half * width, (half + 1) * width)
                scaled = stream_ref[block, 1, :, cols].astype(jnp.float32) * gain_ref[:, cols]
                delta = scaled * inverse_here - hidden_ref[place, cols] * factor_here
                delta_ref[cols, place] = delta.T.astype(jnp.bfloat16)

    multiply(inv_scale, side_ref, delta_ref[...], rows_ref, mine_ref, theirs_ref)


def backward_next_kernel(inv_scale, side_ref, rows_ref, delta_ref, mine_ref, theirs_ref):
    multiply(inv_scale, side_ref, delta_ref[...], rows_ref, mine_ref, theirs_ref)


def backward(side, rows, hidden, gain, sums, stream, inv_scale, features):
    tokens, depth = rows.shape
    block = hidden.shape[1]
    width = block // 2
    step = 256
    steps = depth // step // HALVES
    params = pltpu.CompilerParams(vmem_limit_bytes=VMEM_LIMIT)
    cost = pl.CostEstimate(
        flops=2 * tokens * depth * block // HALVES, bytes_accessed=5 * 1024 * 1024, transcendentals=0
    )
    outs = [
        jax.ShapeDtypeStruct((depth // HALVES, width), jnp.float32),
        jax.ShapeDtypeStruct((depth // HALVES, width), jnp.bfloat16),
    ]
    whole = lambda array: pl.BlockSpec(array.shape, lambda i, *_: (0,) * array.ndim)
    delta = jax.ShapeDtypeStruct((block, tokens), jnp.bfloat16)
    out = pl.BlockSpec((step, width), lambda i, *_: (i, 0))
    *first, delta = pl.pallas_call(
        functools.partial(backward_first_kernel, inv_scale, features),
        grid_spec=pltpu.PrefetchScalarGridSpec(
            num_scalar_prefetch=1,
            grid=(steps,),
            in_specs=[pl.BlockSpec((tokens, step), lambda i, *_: (0, i))]
            + [whole(array) for array in (hidden, gain, sums, stream)],
            out_specs=[out, out, whole(delta)],
        ),
        out_shape=outs + [delta],
        compiler_params=params,
        cost_estimate=cost,
        name="backward_first",
    )(side, rows, hidden, gain, sums, stream)
    result = [first]
    for half in range(1, HALVES):
        result.append(
            pl.pallas_call(
                functools.partial(backward_next_kernel, inv_scale),
                grid_spec=pltpu.PrefetchScalarGridSpec(
                    num_scalar_prefetch=1,
                    grid=(steps,),
                    in_specs=[
                        pl.BlockSpec((tokens, step), lambda i, *_, half=half: (0, half * steps + i)),
                        whole(delta),
                    ],
                    out_specs=[out, out],
                ),
                out_shape=outs,
                compiler_params=params,
                cost_estimate=cost,
                name="backward_next",
            )(side, rows, delta)
        )
    return result


def swap_minor(array):
    return lax.ppermute(array, "minor", [(0, 1), (1, 0)])


def sums_of_all(sums):
    return lax.all_to_all(sums, "major", split_axis=0, concat_axis=0, tiled=True)


def spread_columns(array):
    return lax.all_to_all(array, "column", split_axis=0, concat_axis=0, tiled=True)


def plan_moves(sources):
    planes = lax.axis_size("plane")
    columns = lax.axis_size("column")
    me = lax.axis_index("plane")
    member = jnp.arange(planes * columns, dtype=jnp.int32)
    here, there = member // columns, sources // columns
    offset = lax.rem(here - there + planes, planes)
    earlier = member[None, :] < member[:, None]
    same = (here[None, :] == here[:, None]) & (there[None, :] == there[:, None])
    rank = jnp.sum((earlier & same).astype(jnp.int32), axis=1)
    most = jnp.max(jnp.where(offset > 0, rank, 0))
    targets = jnp.arange(1, planes, dtype=jnp.int32)[:, None, None]
    slots = jnp.arange(columns, dtype=jnp.int32)[None, :, None]
    leaving = (there == me) & (rank == slots)
    column = lax.rem(sources, columns)
    by_shift = jnp.sum(jnp.where(leaving & (offset == targets), column, 0), axis=2)
    mine = lambda values: lax.dynamic_slice_in_dim(values, me * columns, columns)
    return dict(
        column=mine(column),
        offset=mine(offset),
        rank=mine(rank),
        by_shift=by_shift,
        most=most,
    )


def pick(pieces, slots):
    kinds = pieces.shape[0] // lax.axis_size("column")
    return pieces[(slots[:, None] * kinds + jnp.arange(kinds, dtype=jnp.int32)).reshape(-1)]


def send_planes(pieces, slots):
    planes = lax.axis_size("plane")
    return [
        lax.ppermute(pick(pieces, slots[shift - 1]), "plane", [(i, (i + shift) % planes) for i in range(planes)])
        for shift in range(1, planes)
    ]


def choose_kernel(kinds, copies, which_ref, start_ref, *refs):
    refs, out_ref, sems = refs[:-2], refs[-2], refs[-1]
    columns = out_ref.shape[0]
    slot = lambda place, copy: out_ref.at[place, copy] if copies else out_ref.at[place]
    for place in range(columns):
        for number, ref in enumerate(refs):
            @pl.when(which_ref[place] == number)
            def _():
                for copy in range(max(copies, 1)):
                    source = ref.at[pl.ds(start_ref[place], kinds)]
                    pltpu.make_async_copy(source, slot(place, copy), sems.at[place, copy]).start()

    for place in range(columns):
        for copy in range(max(copies, 1)):
            pltpu.make_async_copy(refs[0].at[pl.ds(0, kinds)], slot(place, copy), sems.at[place, copy]).wait()


def choose(pieces, received, which, start, kinds, copies):
    columns = which.shape[0]
    shape = ((columns, copies) if copies else (columns,)) + (kinds,) + pieces.shape[1:]
    anywhere = pl.BlockSpec(memory_space=pl.ANY)
    return pl.pallas_call(
        functools.partial(choose_kernel, kinds, copies),
        grid_spec=pltpu.PrefetchScalarGridSpec(
            num_scalar_prefetch=2,
            grid=(1,),
            in_specs=[anywhere] * (1 + len(received)),
            out_specs=pl.BlockSpec(shape, lambda i, *_: (0,) * len(shape)),
            scratch_shapes=[pltpu.SemaphoreType.DMA((columns, max(copies, 1)))],
        ),
        out_shape=jax.ShapeDtypeStruct(shape, pieces.dtype),
        compiler_params=pltpu.CompilerParams(vmem_limit_bytes=VMEM_LIMIT),
        name="choose",
    )(which, start, pieces, *received)


def across(pieces, received, plan, copies):
    kinds = pieces.shape[0] // lax.axis_size("column")

    def take(pieces, received):
        last = received[0].shape[0] // kinds - 1
        place = jnp.where(plan["offset"] == 0, plan["column"], jnp.minimum(plan["rank"], last))
        return choose(pieces, received, plan["offset"], place * kinds, kinds, copies)

    def all_slots(pieces, received):
        return take(pieces, send_planes(pieces, plan["by_shift"]))

    return lax.cond(plan["most"] >= FEW, all_slots, take, pieces, received)


def local(
    attention_out,
    residual,
    upstream,
    norm_gain,
    weight,
    first_moment,
    second_moment,
    sources,
    rate_index,
):
    columns = lax.axis_size("column")
    minor = lax.axis_index("minor")
    depth, width = weight.shape[1:]
    rows = depth // columns
    features = residual.shape[2]

    gathered = lax.all_gather(attention_out[0], "major", axis=0, tiled=True)
    plan = plan_moves(sources)
    few = plan["by_shift"][:, :FEW]
    gain_other = swap_minor(norm_gain[0])
    gain = jnp.where(
        minor == 0,
        jnp.concatenate((norm_gain[0], gain_other)),
        jnp.concatenate((gain_other, norm_gain[0])),
    ).astype(jnp.float32)[None, :]
    weights = spread_columns(weight[0].reshape(columns, rows, width))
    moments = jnp.stack(
        [array[0].reshape(columns, rows, width) for array in (first_moment, second_moment)], axis=1
    )
    weights, moments, gain = lax.optimization_barrier((weights, moments, gain))
    moments = spread_columns(moments).reshape(columns * (KINDS - 1), rows, width)
    weights_in = send_planes(weights, few)
    weights_in, moments = lax.optimization_barrier((weights_in, moments))
    weights = across(weights, weights_in, plan, MINOR)
    weights, moments = lax.optimization_barrier((weights, moments))
    weights = lax.all_to_all(
        weights.reshape(columns * MINOR, rows, width), ("column", "minor"), split_axis=0, concat_axis=0, tiled=True
    ).reshape(columns, MINOR, rows, width)
    moments_in = send_planes(moments, few)
    stream = pack(residual[0], upstream[0], lax.axis_size("major"))
    weights, stream = lax.optimization_barrier((weights, stream))
    stream = lax.all_to_all(stream, "major", split_axis=0, concat_axis=0, tiled=True)

    inv_scale = 1.0 / math.sqrt(depth)
    side = minor.astype(jnp.int32)[None]
    hidden, sums = forward(gathered, weights, gain, stream, inv_scale)
    moments_in, sums = lax.optimization_barrier((moments_in, sums))
    sums = sums_of_all(sums)
    moments = across(moments, moments_in, plan, 0)
    moments, sums = lax.optimization_barrier((moments, sums))
    moments = spread_columns(moments)
    halves = backward(side, gathered, hidden, gain, sums, stream, inv_scale, features)
    result = []
    for half, (mine, theirs) in enumerate(halves):
        result = adamw(half, side, rate_index, weights, moments, mine, swap_minor(theirs), result)
    return tuple(result)


def solution(mesh):
    members, shards = mesh.devices.shape
    split = Mesh(
        mesh.devices.reshape(PLANES, members // PLANES, shards // MINOR, MINOR),
        ("plane", "column", "major", "minor"),
    )
    member, fsdp = ("plane", "column"), ("major", "minor")
    in_specs = (
        P(member, fsdp, None),
        P(member, fsdp, None),
        P(member, fsdp, None),
        P(member, fsdp),
        P(member, None, fsdp),
        P(member, None, fsdp),
        P(member, None, fsdp),
        P(),
        P(member),
    )
    out_specs = (P(member, None, fsdp),) * 3
    return jax.shard_map(local, mesh=split, in_specs=in_specs, out_specs=out_specs, check_vma=False)
```

```python
import functools
import math

import jax
import jax.numpy as jnp
from jax import lax
from jax.experimental import pallas as pl
from jax.experimental.pallas import tpu as pltpu
from jax.sharding import Mesh
from jax.sharding import PartitionSpec as P

EPS = 1e-06
ADAM_EPS = 1e-08
BETA_ONE = 0.9
BETA_TWO = 0.95
DECAY = 0.1
bias_one = 1.0 - 0.9**10
bias_two = 1.0 - 0.95**10
RATE_TABLE = (0.02, 0.032, 0.05, 0.08, 0.125)
MINOR = 2
PLANES = 4
FEW = 2
LANES = 128
VMEM_LIMIT = 24 * 1024 * 1024
KINDS = 3
HALVES = 2


def adamw_kernel(rate_ref, weight_ref, moments_ref, mine_ref, theirs_ref, *refs):
    weight_out, first_out, second_out = refs[-3:]
    rate = jnp.float32(0.0)
    for slot, value in enumerate(RATE_TABLE):
        rate = jnp.where(rate_ref[0] == slot, jnp.float32(value), rate)
    gradient = mine_ref[...] + theirs_ref[...].astype(jnp.float32)
    weight_now = weight_ref[...].astype(jnp.float32)
    first_now = moments_ref[0, 0].astype(jnp.float32)
    second_now = moments_ref[0, 1].astype(jnp.float32)
    first_sum = BETA_ONE * first_now + (1.0 - BETA_ONE) * gradient
    second_sum = BETA_TWO * second_now + (1.0 - BETA_TWO) * gradient * gradient
    update = first_sum / bias_one / (jnp.sqrt(second_sum / bias_two) + ADAM_EPS)
    weight_new = weight_now * (1.0 - rate * DECAY) - rate * update
    weight_out[0] = weight_new.astype(jnp.bfloat16)
    first_out[0] = first_sum.astype(jnp.bfloat16)
    second_out[0] = second_sum.astype(jnp.bfloat16)


def adamw(half, rate_index, weight, moments, mine, theirs, earlier):
    pieces, _, rows, width = moments.shape
    steps = pieces // HALVES
    first = half * steps
    flat = pl.BlockSpec((rows, width), lambda i, r: (i, 0))
    out = pl.BlockSpec((1, rows, width), lambda i, r: (0, first + i, 0))
    count = len(earlier)
    return pl.pallas_call(
        adamw_kernel,
        grid_spec=pltpu.PrefetchScalarGridSpec(
            num_scalar_prefetch=1,
            grid=(steps,),
            in_specs=[
                pl.BlockSpec((rows, width), lambda i, r: (first + i, 0)),
                pl.BlockSpec((1, KINDS - 1, rows, width), lambda i, r: (first + i, 0, 0, 0)),
                flat,
                flat,
            ]
            + [pl.BlockSpec(memory_space=pl.ANY)] * count,
            out_specs=[out, out, out],
        ),
        out_shape=[jax.ShapeDtypeStruct((1, pieces * rows, width), jnp.bfloat16)] * KINDS,
        input_output_aliases={5 + i: i for i in range(count)},
        compiler_params=pltpu.CompilerParams(vmem_limit_bytes=VMEM_LIMIT),
        cost_estimate=pl.CostEstimate(
            flops=20 * steps * rows * width,
            bytes_accessed=18 * steps * rows * width,
            transcendentals=steps * rows * width,
        ),
        name="adamw",
    )(rate_index, weight, moments, mine, theirs, *earlier)


def pack_kernel(residual_ref, upstream_ref, out_ref):
    out_ref[0, 0] = residual_ref[...]
    out_ref[0, 1] = upstream_ref[...]


def pack(residual, upstream, blocks):
    tokens, features = residual.shape
    block = features // blocks
    columns = pl.BlockSpec((tokens, block), lambda i: (0, i))
    return pl.pallas_call(
        pack_kernel,
        grid=(blocks,),
        in_specs=[columns, columns],
        out_specs=pl.BlockSpec((1, 2, tokens, block), lambda i: (i, 0, 0, 0)),
        out_shape=jax.ShapeDtypeStruct((blocks, 2, tokens, block), residual.dtype),
        compiler_params=pltpu.CompilerParams(vmem_limit_bytes=VMEM_LIMIT),
        name="pack",
    )(residual, upstream)


def forward_kernel(inv_scale, side_ref, rows_ref, own_ref, other_ref, stream_ref, gain_ref, hidden_ref, sums_ref, both_ref):
    width = own_ref.shape[1]

    @pl.when(pl.program_id(0) == 0)
    def _():
        @pl.when(side_ref[0] == 0)
        def _():
            both_ref[:, :width] = own_ref[...]
            both_ref[:, width:] = other_ref[...]

        @pl.when(side_ref[0] != 0)
        def _():
            both_ref[:, :width] = other_ref[...]
            both_ref[:, width:] = own_ref[...]

    linear = jnp.dot(rows_ref[...], both_ref[...], preferred_element_type=jnp.float32)
    count, block = linear.shape
    stream = stream_ref[...]
    resid = stream[:, 0].reshape(count, block).astype(jnp.float32)
    upstream = stream[:, 1].reshape(count, block).astype(jnp.float32)
    hidden = resid + linear * inv_scale
    hidden_ref[...] = hidden
    scaled = upstream * gain_ref[...]
    squares = jnp.sum(hidden * hidden, axis=1, keepdims=True)
    inner = jnp.sum(scaled * hidden, axis=1, keepdims=True)
    lane = lax.broadcasted_iota(jnp.int32, (count, LANES), 1)
    packed = jnp.where(lane == 0, squares, jnp.where(lane == 1, inner, 0.0)).T[:2]
    for target in range(sums_ref.shape[0]):
        sums_ref[target] = packed


def forward(side, rows, own, other, gain, stream, inv_scale):
    tokens, depth = rows.shape
    blocks, _, per, block = stream.shape
    step = 2 * per
    return pl.pallas_call(
        functools.partial(forward_kernel, inv_scale),
        grid_spec=pltpu.PrefetchScalarGridSpec(
            num_scalar_prefetch=1,
            grid=(tokens // step,),
            in_specs=[
                pl.BlockSpec((step, depth), lambda i, m: (i, 0)),
                pl.BlockSpec(own.shape, lambda i, m: (0, 0)),
                pl.BlockSpec(other.shape, lambda i, m: (0, 0)),
                pl.BlockSpec((2, 2, per, block), lambda i, m: (i, 0, 0, 0)),
                pl.BlockSpec(gain.shape, lambda i, m: (0, 0)),
            ],
            out_specs=[
                pl.BlockSpec((step, block), lambda i, m: (i, 0)),
                pl.BlockSpec((blocks, 2, step), lambda i, m: (0, 0, i)),
            ],
            scratch_shapes=[pltpu.VMEM((depth, block), jnp.bfloat16)],
        ),
        out_shape=[
            jax.ShapeDtypeStruct((tokens, block), jnp.float32),
            jax.ShapeDtypeStruct((blocks, 2, tokens), jnp.float32),
        ],
        compiler_params=pltpu.CompilerParams(vmem_limit_bytes=VMEM_LIMIT),
        cost_estimate=pl.CostEstimate(
            flops=2 * tokens * depth * block, bytes_accessed=7 * 1024 * 1024, transcendentals=0
        ),
        name="forward",
    )(side, rows, own, other, stream, gain)


def multiply(inv_scale, side_ref, delta, rows_ref, mine_ref, theirs_ref):
    width = mine_ref.shape[1]
    grad = jnp.dot(delta, rows_ref[...], preferred_element_type=jnp.float32) * inv_scale
    low = grad[:width].T
    high = grad[width:].T
    first = side_ref[0] == 0
    mine_ref[...] = jnp.where(first, low, high)
    theirs_ref[...] = jnp.where(first, high, low).astype(jnp.bfloat16)


def backward_first_kernel(inv_scale, features, side_ref, rows_ref, hidden_ref, gain_ref, sums_ref, stream_ref, mine_ref, theirs_ref, delta_ref):
    width = mine_ref.shape[1]
    blocks, _, per, _ = stream_ref.shape

    @pl.when(pl.program_id(0) == 0)
    def _():
        sums = jnp.sum(sums_ref[...], axis=0)
        inverse = lax.rsqrt(sums[0:1] / features + EPS)
        factor = sums[1:2] / features * (inverse * inverse * inverse)
        for block in range(blocks):
            place = slice(block * per, (block + 1) * per)
            inverse_here = jnp.broadcast_to(inverse[:, place], (LANES, per)).T
            factor_here = jnp.broadcast_to(factor[:, place], (LANES, per)).T
            for half in range(2):
                cols = slice(half * width, (half + 1) * width)
                scaled = stream_ref[block, 1, :, cols].astype(jnp.float32) * gain_ref[:, cols]
                delta = scaled * inverse_here - hidden_ref[place, cols] * factor_here
                delta_ref[cols, place] = delta.T.astype(jnp.bfloat16)

    multiply(inv_scale, side_ref, delta_ref[...], rows_ref, mine_ref, theirs_ref)


def backward_next_kernel(inv_scale, side_ref, rows_ref, delta_ref, mine_ref, theirs_ref):
    multiply(inv_scale, side_ref, delta_ref[...], rows_ref, mine_ref, theirs_ref)


def backward(side, rows, hidden, gain, sums, stream, inv_scale, features):
    tokens, depth = rows.shape
    block = hidden.shape[1]
    width = block // 2
    step = 256
    steps = depth // step // HALVES
    params = pltpu.CompilerParams(vmem_limit_bytes=VMEM_LIMIT)
    cost = pl.CostEstimate(
        flops=2 * tokens * depth * block // HALVES, bytes_accessed=5 * 1024 * 1024, transcendentals=0
    )
    outs = [
        jax.ShapeDtypeStruct((depth // HALVES, width), jnp.float32),
        jax.ShapeDtypeStruct((depth // HALVES, width), jnp.bfloat16),
    ]
    whole = lambda array: pl.BlockSpec(array.shape, lambda i, *_: (0,) * array.ndim)
    delta = jax.ShapeDtypeStruct((block, tokens), jnp.bfloat16)
    out = pl.BlockSpec((step, width), lambda i, *_: (i, 0))
    *first, delta = pl.pallas_call(
        functools.partial(backward_first_kernel, inv_scale, features),
        grid_spec=pltpu.PrefetchScalarGridSpec(
            num_scalar_prefetch=1,
            grid=(steps,),
            in_specs=[pl.BlockSpec((tokens, step), lambda i, *_: (0, i))]
            + [whole(array) for array in (hidden, gain, sums, stream)],
            out_specs=[out, out, whole(delta)],
        ),
        out_shape=outs + [delta],
        compiler_params=params,
        cost_estimate=cost,
        name="backward_first",
    )(side, rows, hidden, gain, sums, stream)
    result = [first]
    for half in range(1, HALVES):
        result.append(
            pl.pallas_call(
                functools.partial(backward_next_kernel, inv_scale),
                grid_spec=pltpu.PrefetchScalarGridSpec(
                    num_scalar_prefetch=1,
                    grid=(steps,),
                    in_specs=[
                        pl.BlockSpec((tokens, step), lambda i, *_, half=half: (0, half * steps + i)),
                        whole(delta),
                    ],
                    out_specs=[out, out],
                ),
                out_shape=outs,
                compiler_params=params,
                cost_estimate=cost,
                name="backward_next",
            )(side, rows, delta)
        )
    return result


def swap_minor(array):
    return lax.ppermute(array, "minor", [(0, 1), (1, 0)])


def sums_of_all(sums):
    return lax.all_to_all(sums, "major", split_axis=0, concat_axis=0, tiled=True)


def spread_columns(array):
    return lax.all_to_all(array, "column", split_axis=0, concat_axis=0, tiled=True)


def plan_moves(sources):
    planes = lax.axis_size("plane")
    columns = lax.axis_size("column")
    me = lax.axis_index("plane")
    member = jnp.arange(planes * columns, dtype=jnp.int32)
    here, there = member // columns, sources // columns
    offset = lax.rem(here - there + planes, planes)
    earlier = member[None, :] < member[:, None]
    same = (here[None, :] == here[:, None]) & (there[None, :] == there[:, None])
    rank = jnp.sum((earlier & same).astype(jnp.int32), axis=1)
    most = jnp.max(jnp.where(offset > 0, rank, 0))
    targets = jnp.arange(1, planes, dtype=jnp.int32)[:, None, None]
    slots = jnp.arange(columns, dtype=jnp.int32)[None, :, None]
    leaving = (there == me) & (rank == slots)
    column = lax.rem(sources, columns)
    by_shift = jnp.sum(jnp.where(leaving & (offset == targets), column, 0), axis=2)
    mine = lambda values: lax.dynamic_slice_in_dim(values, me * columns, columns)
    return dict(
        column=mine(column),
        offset=mine(offset),
        rank=mine(rank),
        by_shift=by_shift,
        most=most,
    )


def pick(pieces, slots):
    kinds = pieces.shape[0] // lax.axis_size("column")
    return pieces[(slots[:, None] * kinds + jnp.arange(kinds, dtype=jnp.int32)).reshape(-1)]


def send_plane(pieces, slots, shift):
    planes = lax.axis_size("plane")
    return lax.ppermute(pick(pieces, slots[shift - 1]), "plane", [(i, (i + shift) % planes) for i in range(planes)])


def send_planes(pieces, slots):
    return [send_plane(pieces, slots, shift) for shift in range(1, lax.axis_size("plane"))]


def choose_kernel(kinds, which_ref, start_ref, *refs):
    refs, out_ref, sems = refs[:-2], refs[-2], refs[-1]
    columns = out_ref.shape[0]
    for place in range(columns):
        for number, ref in enumerate(refs):
            @pl.when(which_ref[place] == number)
            def _():
                source = ref.at[pl.ds(start_ref[place], kinds)]
                pltpu.make_async_copy(source, out_ref.at[place], sems.at[place]).start()

    for place in range(columns):
        pltpu.make_async_copy(refs[0].at[pl.ds(0, kinds)], out_ref.at[place], sems.at[place]).wait()


def choose(pieces, received, which, start, kinds):
    shape = which.shape + (kinds,) + pieces.shape[1:]
    anywhere = pl.BlockSpec(memory_space=pl.ANY)
    return pl.pallas_call(
        functools.partial(choose_kernel, kinds),
        grid_spec=pltpu.PrefetchScalarGridSpec(
            num_scalar_prefetch=2,
            grid=(1,),
            in_specs=[anywhere] * (1 + len(received)),
            out_specs=pl.BlockSpec(shape, lambda i, *_: (0,) * len(shape)),
            scratch_shapes=[pltpu.SemaphoreType.DMA(which.shape)],
        ),
        out_shape=jax.ShapeDtypeStruct(shape, pieces.dtype),
        compiler_params=pltpu.CompilerParams(vmem_limit_bytes=VMEM_LIMIT),
        name="choose",
    )(which, start, pieces, *received)


def across(pieces, received, plan):
    kinds = pieces.shape[0] // lax.axis_size("column")

    def take(pieces, received):
        last = received[0].shape[0] // kinds - 1
        place = jnp.where(plan["offset"] == 0, plan["column"], jnp.minimum(plan["rank"], last))
        return choose(pieces, received, plan["offset"], place * kinds, kinds)

    def all_slots(pieces, received):
        return take(pieces, send_planes(pieces, plan["by_shift"]))

    return lax.cond(plan["most"] >= FEW, all_slots, take, pieces, received)


def local(
    attention_out,
    residual,
    upstream,
    norm_gain,
    weight,
    first_moment,
    second_moment,
    sources,
    rate_index,
):
    columns = lax.axis_size("column")
    minor = lax.axis_index("minor")
    depth, width = weight.shape[1:]
    rows = depth // columns
    features = residual.shape[2]

    gathered = lax.all_gather(attention_out[0], "major", axis=0, tiled=True)
    plan = plan_moves(sources)
    few = plan["by_shift"][:, :FEW]
    weights = spread_columns(weight[0].reshape(columns, rows, width))
    moments = jnp.stack(
        [array[0].reshape(columns, rows, width) for array in (first_moment, second_moment)], axis=1
    )
    weights, moments = lax.optimization_barrier((weights, moments))
    moments = spread_columns(moments).reshape(columns * (KINDS - 1), rows, width)
    weights_in = send_planes(weights, few)
    weights_in, moments = lax.optimization_barrier((weights_in, moments))
    weights = across(weights, weights_in, plan)
    weights, moments = lax.optimization_barrier((weights, moments))
    weights = spread_columns(weights.reshape(columns, rows, width))
    gain_other = swap_minor(norm_gain[0])
    gain = jnp.where(
        minor == 0,
        jnp.concatenate((norm_gain[0], gain_other)),
        jnp.concatenate((gain_other, norm_gain[0])),
    ).astype(jnp.float32)[None, :]
    stream = pack(residual[0], upstream[0], lax.axis_size("major"))
    weights, stream, gain = lax.optimization_barrier((weights, stream, gain))
    stream = lax.all_to_all(stream, "major", split_axis=0, concat_axis=0, tiled=True)
    weights = weights.reshape(depth, width)
    weights_other = swap_minor(weights)
    moments_near = send_plane(moments, few, 1)
    weights_other, moments = lax.optimization_barrier((weights_other, moments))
    moments_in = [moments_near] + [send_plane(moments, few, shift) for shift in range(2, PLANES)]

    inv_scale = 1.0 / math.sqrt(depth)
    side = minor.astype(jnp.int32)[None]
    hidden, sums = forward(side, gathered, weights, weights_other, gain, stream, inv_scale)
    moments_in, sums = lax.optimization_barrier((moments_in, sums))
    sums = sums_of_all(sums)
    moments = across(moments, moments_in, plan)
    moments, sums = lax.optimization_barrier((moments, sums))
    moments = spread_columns(moments)
    halves = backward(side, gathered, hidden, gain, sums, stream, inv_scale, features)
    result = []
    for half, (mine, theirs) in enumerate(halves):
        result = adamw(half, rate_index, weights, moments, mine, swap_minor(theirs), result)
    return tuple(result)


def solution(mesh):
    members, shards = mesh.devices.shape
    split = Mesh(
        mesh.devices.reshape(PLANES, members // PLANES, shards // MINOR, MINOR),
        ("plane", "column", "major", "minor"),
    )
    member, fsdp = ("plane", "column"), ("major", "minor")
    in_specs = (
        P(member, fsdp, None),
        P(member, fsdp, None),
        P(member, fsdp, None),
        P(member, fsdp),
        P(member, None, fsdp),
        P(member, None, fsdp),
        P(member, None, fsdp),
        P(),
        P(member),
    )
    out_specs = (P(member, None, fsdp),) * 3
    return jax.shard_map(local, mesh=split, in_specs=in_specs, out_specs=out_specs, check_vma=False)
```

```python
import functools
import math

import jax
import jax.numpy as jnp
from jax import lax
from jax.experimental import pallas as pl
from jax.experimental.pallas import tpu as pltpu
from jax.sharding import Mesh
from jax.sharding import PartitionSpec as P

EPS = 1e-06
ADAM_EPS = 1e-08
BETA_ONE = 0.9
BETA_TWO = 0.95
DECAY = 0.1
bias_one = 1.0 - 0.9**10
bias_two = 1.0 - 0.95**10
RATE_TABLE = (0.02, 0.032, 0.05, 0.08, 0.125)
MINOR = 2
PLANES = 4
FEW = 2
LANES = 128
VMEM_LIMIT = 24 * 1024 * 1024
KINDS = 3
HALVES = 2


def adamw_kernel(rate_ref, weight_ref, moments_ref, mine_ref, theirs_ref, *refs):
    weight_out, first_out, second_out = refs[-3:]
    rate = jnp.float32(0.0)
    for slot, value in enumerate(RATE_TABLE):
        rate = jnp.where(rate_ref[0] == slot, jnp.float32(value), rate)
    gradient = mine_ref[...] + theirs_ref[...].astype(jnp.float32)
    weight_now = weight_ref[...].astype(jnp.float32)
    first_now = moments_ref[0, 0].astype(jnp.float32)
    second_now = moments_ref[0, 1].astype(jnp.float32)
    first_sum = BETA_ONE * first_now + (1.0 - BETA_ONE) * gradient
    second_sum = BETA_TWO * second_now + (1.0 - BETA_TWO) * gradient * gradient
    update = first_sum / bias_one / (jnp.sqrt(second_sum / bias_two) + ADAM_EPS)
    weight_new = weight_now * (1.0 - rate * DECAY) - rate * update
    weight_out[0] = weight_new.astype(jnp.bfloat16)
    first_out[0] = first_sum.astype(jnp.bfloat16)
    second_out[0] = second_sum.astype(jnp.bfloat16)


def adamw(half, rate_index, weight, moments, mine, theirs, earlier):
    pieces, _, rows, width = moments.shape
    steps = pieces // HALVES
    first = half * steps
    flat = pl.BlockSpec((rows, width), lambda i, r: (i, 0))
    out = pl.BlockSpec((1, rows, width), lambda i, r: (0, first + i, 0))
    count = len(earlier)
    return pl.pallas_call(
        adamw_kernel,
        grid_spec=pltpu.PrefetchScalarGridSpec(
            num_scalar_prefetch=1,
            grid=(steps,),
            in_specs=[
                pl.BlockSpec((rows, width), lambda i, r: (first + i, 0)),
                pl.BlockSpec((1, KINDS - 1, rows, width), lambda i, r: (first + i, 0, 0, 0)),
                flat,
                flat,
            ]
            + [pl.BlockSpec(memory_space=pl.ANY)] * count,
            out_specs=[out, out, out],
        ),
        out_shape=[jax.ShapeDtypeStruct((1, pieces * rows, width), jnp.bfloat16)] * KINDS,
        input_output_aliases={5 + i: i for i in range(count)},
        compiler_params=pltpu.CompilerParams(vmem_limit_bytes=VMEM_LIMIT),
        cost_estimate=pl.CostEstimate(
            flops=20 * steps * rows * width,
            bytes_accessed=18 * steps * rows * width,
            transcendentals=steps * rows * width,
        ),
        name="adamw",
    )(rate_index, weight, moments, mine, theirs, *earlier)


def pack_kernel(residual_ref, upstream_ref, out_ref):
    out_ref[0, 0] = residual_ref[...]
    out_ref[0, 1] = upstream_ref[...]


def pack(residual, upstream, blocks):
    tokens, features = residual.shape
    block = features // blocks
    columns = pl.BlockSpec((tokens, block), lambda i: (0, i))
    return pl.pallas_call(
        pack_kernel,
        grid=(blocks,),
        in_specs=[columns, columns],
        out_specs=pl.BlockSpec((1, 2, tokens, block), lambda i: (i, 0, 0, 0)),
        out_shape=jax.ShapeDtypeStruct((blocks, 2, tokens, block), residual.dtype),
        compiler_params=pltpu.CompilerParams(vmem_limit_bytes=VMEM_LIMIT),
        name="pack",
    )(residual, upstream)


def forward_kernel(inv_scale, side_ref, rows_ref, own_ref, other_ref, stream_ref, gain_ref, hidden_ref, sums_ref, both_ref):
    width = own_ref.shape[1]

    @pl.when(pl.program_id(0) == 0)
    def _():
        @pl.when(side_ref[0] == 0)
        def _():
            both_ref[:, :width] = own_ref[...]
            both_ref[:, width:] = other_ref[...]

        @pl.when(side_ref[0] != 0)
        def _():
            both_ref[:, :width] = other_ref[...]
            both_ref[:, width:] = own_ref[...]

    linear = jnp.dot(rows_ref[...], both_ref[...], preferred_element_type=jnp.float32)
    count, block = linear.shape
    stream = stream_ref[...]
    resid = stream[:, 0].reshape(count, block).astype(jnp.float32)
    upstream = stream[:, 1].reshape(count, block).astype(jnp.float32)
    hidden = resid + linear * inv_scale
    hidden_ref[...] = hidden
    scaled = upstream * gain_ref[...]
    squares = jnp.sum(hidden * hidden, axis=1, keepdims=True)
    inner = jnp.sum(scaled * hidden, axis=1, keepdims=True)
    lane = lax.broadcasted_iota(jnp.int32, (count, LANES), 1)
    packed = jnp.where(lane == 0, squares, jnp.where(lane == 1, inner, 0.0)).T[:2]
    for target in range(sums_ref.shape[0]):
        sums_ref[target] = packed


def forward(side, rows, own, other, gain, stream, inv_scale):
    tokens, depth = rows.shape
    blocks, _, per, block = stream.shape
    step = 2 * per
    return pl.pallas_call(
        functools.partial(forward_kernel, inv_scale),
        grid_spec=pltpu.PrefetchScalarGridSpec(
            num_scalar_prefetch=1,
            grid=(tokens // step,),
            in_specs=[
                pl.BlockSpec((step, depth), lambda i, m: (i, 0)),
                pl.BlockSpec(own.shape, lambda i, m: (0, 0)),
                pl.BlockSpec(other.shape, lambda i, m: (0, 0)),
                pl.BlockSpec((2, 2, per, block), lambda i, m: (i, 0, 0, 0)),
                pl.BlockSpec(gain.shape, lambda i, m: (0, 0)),
            ],
            out_specs=[
                pl.BlockSpec((step, block), lambda i, m: (i, 0)),
                pl.BlockSpec((blocks, 2, step), lambda i, m: (0, 0, i)),
            ],
            scratch_shapes=[pltpu.VMEM((depth, block), jnp.bfloat16)],
        ),
        out_shape=[
            jax.ShapeDtypeStruct((tokens, block), jnp.float32),
            jax.ShapeDtypeStruct((blocks, 2, tokens), jnp.float32),
        ],
        compiler_params=pltpu.CompilerParams(vmem_limit_bytes=VMEM_LIMIT),
        cost_estimate=pl.CostEstimate(
            flops=2 * tokens * depth * block, bytes_accessed=7 * 1024 * 1024, transcendentals=0
        ),
        name="forward",
    )(side, rows, own, other, stream, gain)


def multiply(inv_scale, side_ref, delta, rows_ref, mine_ref, theirs_ref):
    width = mine_ref.shape[1]
    grad = jnp.dot(delta, rows_ref[...], preferred_element_type=jnp.float32) * inv_scale
    low = grad[:width].T
    high = grad[width:].T
    first = side_ref[0] == 0
    mine_ref[...] = jnp.where(first, low, high)
    theirs_ref[...] = jnp.where(first, high, low).astype(jnp.bfloat16)


def backward_first_kernel(inv_scale, features, side_ref, rows_ref, hidden_ref, gain_ref, sums_ref, stream_ref, mine_ref, theirs_ref, delta_ref):
    width = mine_ref.shape[1]
    blocks, _, per, _ = stream_ref.shape

    @pl.when(pl.program_id(0) == 0)
    def _():
        sums = jnp.sum(sums_ref[...], axis=0)
        inverse = lax.rsqrt(sums[0:1] / features + EPS)
        factor = sums[1:2] / features * (inverse * inverse * inverse)
        for block in range(blocks):
            place = slice(block * per, (block + 1) * per)
            inverse_here = jnp.broadcast_to(inverse[:, place], (LANES, per)).T
            factor_here = jnp.broadcast_to(factor[:, place], (LANES, per)).T
            for half in range(2):
                cols = slice(half * width, (half + 1) * width)
                scaled = stream_ref[block, 1, :, cols].astype(jnp.float32) * gain_ref[:, cols]
                delta = scaled * inverse_here - hidden_ref[place, cols] * factor_here
                delta_ref[cols, place] = delta.T.astype(jnp.bfloat16)

    multiply(inv_scale, side_ref, delta_ref[...], rows_ref, mine_ref, theirs_ref)


def backward_next_kernel(inv_scale, side_ref, rows_ref, delta_ref, mine_ref, theirs_ref):
    multiply(inv_scale, side_ref, delta_ref[...], rows_ref, mine_ref, theirs_ref)


def backward(side, rows, hidden, gain, sums, stream, inv_scale, features):
    tokens, depth = rows.shape
    block = hidden.shape[1]
    width = block // 2
    step = 256
    steps = depth // step // HALVES
    params = pltpu.CompilerParams(vmem_limit_bytes=VMEM_LIMIT)
    cost = pl.CostEstimate(
        flops=2 * tokens * depth * block // HALVES, bytes_accessed=5 * 1024 * 1024, transcendentals=0
    )
    outs = [
        jax.ShapeDtypeStruct((depth // HALVES, width), jnp.float32),
        jax.ShapeDtypeStruct((depth // HALVES, width), jnp.bfloat16),
    ]
    whole = lambda array: pl.BlockSpec(array.shape, lambda i, *_: (0,) * array.ndim)
    delta = jax.ShapeDtypeStruct((block, tokens), jnp.bfloat16)
    out = pl.BlockSpec((step, width), lambda i, *_: (i, 0))
    *first, delta = pl.pallas_call(
        functools.partial(backward_first_kernel, inv_scale, features),
        grid_spec=pltpu.PrefetchScalarGridSpec(
            num_scalar_prefetch=1,
            grid=(steps,),
            in_specs=[pl.BlockSpec((tokens, step), lambda i, *_: (0, i))]
            + [whole(array) for array in (hidden, gain, sums, stream)],
            out_specs=[out, out, whole(delta)],
        ),
        out_shape=outs + [delta],
        compiler_params=params,
        cost_estimate=cost,
        name="backward_first",
    )(side, rows, hidden, gain, sums, stream)
    result = [first]
    for half in range(1, HALVES):
        result.append(
            pl.pallas_call(
                functools.partial(backward_next_kernel, inv_scale),
                grid_spec=pltpu.PrefetchScalarGridSpec(
                    num_scalar_prefetch=1,
                    grid=(steps,),
                    in_specs=[
                        pl.BlockSpec((tokens, step), lambda i, *_, half=half: (0, half * steps + i)),
                        whole(delta),
                    ],
                    out_specs=[out, out],
                ),
                out_shape=outs,
                compiler_params=params,
                cost_estimate=cost,
                name="backward_next",
            )(side, rows, delta)
        )
    return result


def swap_minor(array):
    return lax.ppermute(array, "minor", [(0, 1), (1, 0)])


def sums_of_all(sums):
    return lax.all_to_all(sums, "major", split_axis=0, concat_axis=0, tiled=True)


def spread_columns(array):
    return lax.all_to_all(array, "column", split_axis=0, concat_axis=0, tiled=True)


def plan_moves(sources):
    planes = lax.axis_size("plane")
    columns = lax.axis_size("column")
    me = lax.axis_index("plane")
    member = jnp.arange(planes * columns, dtype=jnp.int32)
    here, there = member // columns, sources // columns
    offset = lax.rem(here - there + planes, planes)
    earlier = member[None, :] < member[:, None]
    same = (here[None, :] == here[:, None]) & (there[None, :] == there[:, None])
    rank = jnp.sum((earlier & same).astype(jnp.int32), axis=1)
    most = jnp.max(jnp.where(offset > 0, rank, 0))
    targets = jnp.arange(1, planes, dtype=jnp.int32)[:, None, None]
    slots = jnp.arange(columns, dtype=jnp.int32)[None, :, None]
    leaving = (there == me) & (rank == slots)
    column = lax.rem(sources, columns)
    by_shift = jnp.sum(jnp.where(leaving & (offset == targets), column, 0), axis=2)
    mine = lambda values: lax.dynamic_slice_in_dim(values, me * columns, columns)
    return dict(
        column=mine(column),
        offset=mine(offset),
        rank=mine(rank),
        by_shift=by_shift,
        most=most,
    )


def pick(pieces, slots):
    kinds = pieces.shape[0] // lax.axis_size("column")
    return pieces[(slots[:, None] * kinds + jnp.arange(kinds, dtype=jnp.int32)).reshape(-1)]


def send_plane(pieces, slots, shift):
    planes = lax.axis_size("plane")
    return lax.ppermute(pick(pieces, slots[shift - 1]), "plane", [(i, (i + shift) % planes) for i in range(planes)])


def send_planes(pieces, slots):
    return [send_plane(pieces, slots, shift) for shift in range(1, lax.axis_size("plane"))]


def choose_kernel(kinds, which_ref, start_ref, *refs):
    refs, out_ref, sems = refs[:-2], refs[-2], refs[-1]
    columns = out_ref.shape[0]
    for place in range(columns):
        for number, ref in enumerate(refs):
            @pl.when(which_ref[place] == number)
            def _():
                source = ref.at[pl.ds(start_ref[place], kinds)]
                pltpu.make_async_copy(source, out_ref.at[place], sems.at[place]).start()

    for place in range(columns):
        pltpu.make_async_copy(refs[0].at[pl.ds(0, kinds)], out_ref.at[place], sems.at[place]).wait()


def choose(pieces, received, which, start, kinds):
    shape = which.shape + (kinds,) + pieces.shape[1:]
    anywhere = pl.BlockSpec(memory_space=pl.ANY)
    return pl.pallas_call(
        functools.partial(choose_kernel, kinds),
        grid_spec=pltpu.PrefetchScalarGridSpec(
            num_scalar_prefetch=2,
            grid=(1,),
            in_specs=[anywhere] * (1 + len(received)),
            out_specs=pl.BlockSpec(shape, lambda i, *_: (0,) * len(shape)),
            scratch_shapes=[pltpu.SemaphoreType.DMA(which.shape)],
        ),
        out_shape=jax.ShapeDtypeStruct(shape, pieces.dtype),
        compiler_params=pltpu.CompilerParams(vmem_limit_bytes=VMEM_LIMIT),
        name="choose",
    )(which, start, pieces, *received)


def across(pieces, received, plan):
    kinds = pieces.shape[0] // lax.axis_size("column")

    def take(pieces, received):
        last = received[0].shape[0] // kinds - 1
        place = jnp.where(plan["offset"] == 0, plan["column"], jnp.minimum(plan["rank"], last))
        return choose(pieces, received, plan["offset"], place * kinds, kinds)

    def all_slots(pieces, received):
        return take(pieces, send_planes(pieces, plan["by_shift"]))

    return lax.cond(plan["most"] >= FEW, all_slots, take, pieces, received)


def local(
    attention_out,
    residual,
    upstream,
    norm_gain,
    weight,
    first_moment,
    second_moment,
    sources,
    rate_index,
):
    columns = lax.axis_size("column")
    minor = lax.axis_index("minor")
    depth, width = weight.shape[1:]
    rows = depth // columns
    features = residual.shape[2]

    gathered = lax.all_gather(attention_out[0], "major", axis=0, tiled=True)
    plan = plan_moves(sources)
    few = plan["by_shift"][:, :FEW]
    weights = spread_columns(weight[0].reshape(columns, rows, width))
    moments = jnp.stack(
        [array[0].reshape(columns, rows, width) for array in (first_moment, second_moment)], axis=1
    )
    weights, moments = lax.optimization_barrier((weights, moments))
    moments = spread_columns(moments).reshape(columns * (KINDS - 1), rows, width)
    weights_in = send_planes(weights, few)
    weights_in, moments = lax.optimization_barrier((weights_in, moments))
    weights = across(weights, weights_in, plan)
    weights, moments = lax.optimization_barrier((weights, moments))
    weights = spread_columns(weights.reshape(columns, rows, width))
    gain_other = swap_minor(norm_gain[0])
    gain = jnp.where(
        minor == 0,
        jnp.concatenate((norm_gain[0], gain_other)),
        jnp.concatenate((gain_other, norm_gain[0])),
    ).astype(jnp.float32)[None, :]
    stream = pack(residual[0], upstream[0], lax.axis_size("major"))
    weights, stream, gain = lax.optimization_barrier((weights, stream, gain))
    stream = lax.all_to_all(stream, "major", split_axis=0, concat_axis=0, tiled=True)
    weights = weights.reshape(depth, width)
    weights_other = swap_minor(weights)
    moments_in = send_planes(moments, few)

    inv_scale = 1.0 / math.sqrt(depth)
    side = minor.astype(jnp.int32)[None]
    hidden, sums = forward(side, gathered, weights, weights_other, gain, stream, inv_scale)
    moments, sums = lax.optimization_barrier((moments, sums))
    sums = sums_of_all(sums)
    moments = across(moments, moments_in, plan)
    moments, sums = lax.optimization_barrier((moments, sums))
    moments = spread_columns(moments)
    halves = backward(side, gathered, hidden, gain, sums, stream, inv_scale, features)
    result = []
    for half, (mine, theirs) in enumerate(halves):
        result = adamw(half, rate_index, weights, moments, mine, swap_minor(theirs), result)
    return tuple(result)


def solution(mesh):
    members, shards = mesh.devices.shape
    split = Mesh(
        mesh.devices.reshape(PLANES, members // PLANES, shards // MINOR, MINOR),
        ("plane", "column", "major", "minor"),
    )
    member, fsdp = ("plane", "column"), ("major", "minor")
    in_specs = (
        P(member, fsdp, None),
        P(member, fsdp, None),
        P(member, fsdp, None),
        P(member, fsdp),
        P(member, None, fsdp),
        P(member, None, fsdp),
        P(member, None, fsdp),
        P(),
        P(member),
    )
    out_specs = (P(member, None, fsdp),) * 3
    return jax.shard_map(local, mesh=split, in_specs=in_specs, out_specs=out_specs, check_vma=False)
```

```python
import functools
import math

import jax
import jax.numpy as jnp
from jax import lax
from jax.experimental import pallas as pl
from jax.experimental.pallas import tpu as pltpu
from jax.sharding import Mesh
from jax.sharding import PartitionSpec as P

EPS = 1e-06
ADAM_EPS = 1e-08
BETA_ONE = 0.9
BETA_TWO = 0.95
DECAY = 0.1
bias_one = 1.0 - 0.9**10
bias_two = 1.0 - 0.95**10
RATE_TABLE = (0.02, 0.032, 0.05, 0.08, 0.125)
MINOR = 2
PLANES = 4
FEW = 2
LANES = 128
VMEM_LIMIT = 24 * 1024 * 1024
KINDS = 3
HALVES = 2


def adamw_kernel(rate_ref, weight_ref, moments_ref, mine_ref, theirs_ref, *refs):
    weight_out, first_out, second_out = refs[-3:]
    rate = jnp.float32(0.0)
    for slot, value in enumerate(RATE_TABLE):
        rate = jnp.where(rate_ref[0] == slot, jnp.float32(value), rate)
    gradient = mine_ref[...] + theirs_ref[...].astype(jnp.float32)
    weight_now = weight_ref[...].astype(jnp.float32)
    first_now = moments_ref[0, 0].astype(jnp.float32)
    second_now = moments_ref[0, 1].astype(jnp.float32)
    first_sum = BETA_ONE * first_now + (1.0 - BETA_ONE) * gradient
    second_sum = BETA_TWO * second_now + (1.0 - BETA_TWO) * gradient * gradient
    update = first_sum / bias_one / (jnp.sqrt(second_sum / bias_two) + ADAM_EPS)
    weight_new = weight_now * (1.0 - rate * DECAY) - rate * update
    weight_out[0] = weight_new.astype(jnp.bfloat16)
    first_out[0] = first_sum.astype(jnp.bfloat16)
    second_out[0] = second_sum.astype(jnp.bfloat16)


def adamw(half, rate_index, weight, moments, mine, theirs, earlier):
    pieces, _, rows, width = moments.shape
    steps = pieces // HALVES
    first = half * steps
    flat = pl.BlockSpec((rows, width), lambda i, r: (i, 0))
    out = pl.BlockSpec((1, rows, width), lambda i, r: (0, first + i, 0))
    count = len(earlier)
    return pl.pallas_call(
        adamw_kernel,
        grid_spec=pltpu.PrefetchScalarGridSpec(
            num_scalar_prefetch=1,
            grid=(steps,),
            in_specs=[
                pl.BlockSpec((rows, width), lambda i, r: (first + i, 0)),
                pl.BlockSpec((1, KINDS - 1, rows, width), lambda i, r: (first + i, 0, 0, 0)),
                flat,
                flat,
            ]
            + [pl.BlockSpec(memory_space=pl.ANY)] * count,
            out_specs=[out, out, out],
        ),
        out_shape=[jax.ShapeDtypeStruct((1, pieces * rows, width), jnp.bfloat16)] * KINDS,
        input_output_aliases={5 + i: i for i in range(count)},
        compiler_params=pltpu.CompilerParams(vmem_limit_bytes=VMEM_LIMIT),
        cost_estimate=pl.CostEstimate(
            flops=20 * steps * rows * width,
            bytes_accessed=18 * steps * rows * width,
            transcendentals=steps * rows * width,
        ),
        name="adamw",
    )(rate_index, weight, moments, mine, theirs, *earlier)


def pack_kernel(residual_ref, upstream_ref, out_ref):
    out_ref[0, 0] = residual_ref[...]
    out_ref[0, 1] = upstream_ref[...]


def pack(residual, upstream, blocks):
    tokens, features = residual.shape
    block = features // blocks
    columns = pl.BlockSpec((tokens, block), lambda i: (0, i))
    return pl.pallas_call(
        pack_kernel,
        grid=(blocks,),
        in_specs=[columns, columns],
        out_specs=pl.BlockSpec((1, 2, tokens, block), lambda i: (i, 0, 0, 0)),
        out_shape=jax.ShapeDtypeStruct((blocks, 2, tokens, block), residual.dtype),
        compiler_params=pltpu.CompilerParams(vmem_limit_bytes=VMEM_LIMIT),
        name="pack",
    )(residual, upstream)


def forward_kernel(inv_scale, side_ref, rows_ref, own_ref, other_ref, stream_ref, gain_ref, hidden_ref, sums_ref, both_ref):
    width = own_ref.shape[1]

    @pl.when(pl.program_id(0) == 0)
    def _():
        @pl.when(side_ref[0] == 0)
        def _():
            both_ref[:, :width] = own_ref[...]
            both_ref[:, width:] = other_ref[...]

        @pl.when(side_ref[0] != 0)
        def _():
            both_ref[:, :width] = other_ref[...]
            both_ref[:, width:] = own_ref[...]

    linear = jnp.dot(rows_ref[...], both_ref[...], preferred_element_type=jnp.float32)
    count, block = linear.shape
    stream = stream_ref[...]
    resid = stream[:, 0].reshape(count, block).astype(jnp.float32)
    upstream = stream[:, 1].reshape(count, block).astype(jnp.float32)
    hidden = resid + linear * inv_scale
    hidden_ref[...] = hidden
    scaled = upstream * gain_ref[...]
    squares = jnp.sum(hidden * hidden, axis=1, keepdims=True)
    inner = jnp.sum(scaled * hidden, axis=1, keepdims=True)
    lane = lax.broadcasted_iota(jnp.int32, (count, LANES), 1)
    packed = jnp.where(lane == 0, squares, jnp.where(lane == 1, inner, 0.0)).T[:2]
    for target in range(sums_ref.shape[0]):
        sums_ref[target] = packed


def forward(side, rows, own, other, gain, stream, inv_scale):
    tokens, depth = rows.shape
    blocks, _, per, block = stream.shape
    step = 2 * per
    return pl.pallas_call(
        functools.partial(forward_kernel, inv_scale),
        grid_spec=pltpu.PrefetchScalarGridSpec(
            num_scalar_prefetch=1,
            grid=(tokens // step,),
            in_specs=[
                pl.BlockSpec((step, depth), lambda i, m: (i, 0)),
                pl.BlockSpec(own.shape, lambda i, m: (0, 0)),
                pl.BlockSpec(other.shape, lambda i, m: (0, 0)),
                pl.BlockSpec((2, 2, per, block), lambda i, m: (i, 0, 0, 0)),
                pl.BlockSpec(gain.shape, lambda i, m: (0, 0)),
            ],
            out_specs=[
                pl.BlockSpec((step, block), lambda i, m: (i, 0)),
                pl.BlockSpec((blocks, 2, step), lambda i, m: (0, 0, i)),
            ],
            scratch_shapes=[pltpu.VMEM((depth, block), jnp.bfloat16)],
        ),
        out_shape=[
            jax.ShapeDtypeStruct((tokens, block), jnp.float32),
            jax.ShapeDtypeStruct((blocks, 2, tokens), jnp.float32),
        ],
        compiler_params=pltpu.CompilerParams(vmem_limit_bytes=VMEM_LIMIT),
        cost_estimate=pl.CostEstimate(
            flops=2 * tokens * depth * block, bytes_accessed=7 * 1024 * 1024, transcendentals=0
        ),
        name="forward",
    )(side, rows, own, other, stream, gain)


def multiply(inv_scale, side_ref, delta, rows_ref, mine_ref, theirs_ref):
    width = mine_ref.shape[1]
    grad = jnp.dot(delta, rows_ref[...], preferred_element_type=jnp.float32) * inv_scale
    low = grad[:width].T
    high = grad[width:].T
    first = side_ref[0] == 0
    mine_ref[...] = jnp.where(first, low, high)
    theirs_ref[...] = jnp.where(first, high, low).astype(jnp.bfloat16)


def backward_first_kernel(inv_scale, features, side_ref, rows_ref, hidden_ref, gain_ref, sums_ref, stream_ref, mine_ref, theirs_ref, delta_ref):
    width = mine_ref.shape[1]
    blocks, _, per, _ = stream_ref.shape

    @pl.when(pl.program_id(0) == 0)
    def _():
        sums = jnp.sum(sums_ref[...], axis=0)
        inverse = lax.rsqrt(sums[0:1] / features + EPS)
        factor = sums[1:2] / features * (inverse * inverse * inverse)
        for block in range(blocks):
            place = slice(block * per, (block + 1) * per)
            inverse_here = jnp.broadcast_to(inverse[:, place], (LANES, per)).T
            factor_here = jnp.broadcast_to(factor[:, place], (LANES, per)).T
            for half in range(2):
                cols = slice(half * width, (half + 1) * width)
                scaled = stream_ref[block, 1, :, cols].astype(jnp.float32) * gain_ref[:, cols]
                delta = scaled * inverse_here - hidden_ref[place, cols] * factor_here
                delta_ref[cols, place] = delta.T.astype(jnp.bfloat16)

    multiply(inv_scale, side_ref, delta_ref[...], rows_ref, mine_ref, theirs_ref)


def backward_next_kernel(inv_scale, side_ref, rows_ref, delta_ref, mine_ref, theirs_ref):
    multiply(inv_scale, side_ref, delta_ref[...], rows_ref, mine_ref, theirs_ref)


def backward(side, rows, hidden, gain, sums, stream, inv_scale, features):
    tokens, depth = rows.shape
    block = hidden.shape[1]
    width = block // 2
    step = 256
    steps = depth // step // HALVES
    params = pltpu.CompilerParams(vmem_limit_bytes=VMEM_LIMIT)
    cost = pl.CostEstimate(
        flops=2 * tokens * depth * block // HALVES, bytes_accessed=5 * 1024 * 1024, transcendentals=0
    )
    outs = [
        jax.ShapeDtypeStruct((depth // HALVES, width), jnp.float32),
        jax.ShapeDtypeStruct((depth // HALVES, width), jnp.bfloat16),
    ]
    whole = lambda array: pl.BlockSpec(array.shape, lambda i, *_: (0,) * array.ndim)
    delta = jax.ShapeDtypeStruct((block, tokens), jnp.bfloat16)
    out = pl.BlockSpec((step, width), lambda i, *_: (i, 0))
    *first, delta = pl.pallas_call(
        functools.partial(backward_first_kernel, inv_scale, features),
        grid_spec=pltpu.PrefetchScalarGridSpec(
            num_scalar_prefetch=1,
            grid=(steps,),
            in_specs=[pl.BlockSpec((tokens, step), lambda i, *_: (0, i))]
            + [whole(array) for array in (hidden, gain, sums, stream)],
            out_specs=[out, out, whole(delta)],
        ),
        out_shape=outs + [delta],
        compiler_params=params,
        cost_estimate=cost,
        name="backward_first",
    )(side, rows, hidden, gain, sums, stream)
    result = [first]
    for half in range(1, HALVES):
        result.append(
            pl.pallas_call(
                functools.partial(backward_next_kernel, inv_scale),
                grid_spec=pltpu.PrefetchScalarGridSpec(
                    num_scalar_prefetch=1,
                    grid=(steps,),
                    in_specs=[
                        pl.BlockSpec((tokens, step), lambda i, *_, half=half: (0, half * steps + i)),
                        whole(delta),
                    ],
                    out_specs=[out, out],
                ),
                out_shape=outs,
                compiler_params=params,
                cost_estimate=cost,
                name="backward_next",
            )(side, rows, delta)
        )
    return result


def swap_minor(array):
    return lax.ppermute(array, "minor", [(0, 1), (1, 0)])


def sums_of_all(sums):
    return lax.all_to_all(sums, "major", split_axis=0, concat_axis=0, tiled=True)


def spread_columns(array):
    return lax.all_to_all(array, "column", split_axis=0, concat_axis=0, tiled=True)


def plan_moves(sources):
    planes = lax.axis_size("plane")
    columns = lax.axis_size("column")
    me = lax.axis_index("plane")
    member = jnp.arange(planes * columns, dtype=jnp.int32)
    here, there = member // columns, sources // columns
    offset = lax.rem(here - there + planes, planes)
    earlier = member[None, :] < member[:, None]
    same = (here[None, :] == here[:, None]) & (there[None, :] == there[:, None])
    rank = jnp.sum((earlier & same).astype(jnp.int32), axis=1)
    most = jnp.max(jnp.where(offset > 0, rank, 0))
    targets = jnp.arange(1, planes, dtype=jnp.int32)[:, None, None]
    slots = jnp.arange(columns, dtype=jnp.int32)[None, :, None]
    leaving = (there == me) & (rank == slots)
    column = lax.rem(sources, columns)
    by_shift = jnp.sum(jnp.where(leaving & (offset == targets), column, 0), axis=2)
    mine = lambda values: lax.dynamic_slice_in_dim(values, me * columns, columns)
    return dict(
        column=mine(column),
        offset=mine(offset),
        rank=mine(rank),
        by_shift=by_shift,
        most=most,
    )


def pick(pieces, slots):
    kinds = pieces.shape[0] // lax.axis_size("column")
    return pieces[(slots[:, None] * kinds + jnp.arange(kinds, dtype=jnp.int32)).reshape(-1)]


def send_plane(pieces, slots, shift):
    planes = lax.axis_size("plane")
    return lax.ppermute(pick(pieces, slots[shift - 1]), "plane", [(i, (i + shift) % planes) for i in range(planes)])


def send_planes(pieces, slots):
    return [send_plane(pieces, slots, shift) for shift in range(1, lax.axis_size("plane"))]


def choose_kernel(kinds, which_ref, start_ref, *refs):
    refs, out_ref, sems = refs[:-2], refs[-2], refs[-1]
    columns = out_ref.shape[0]
    for place in range(columns):
        for number, ref in enumerate(refs):
            @pl.when(which_ref[place] == number)
            def _():
                source = ref.at[pl.ds(start_ref[place], kinds)]
                pltpu.make_async_copy(source, out_ref.at[place], sems.at[place]).start()

    for place in range(columns):
        pltpu.make_async_copy(refs[0].at[pl.ds(0, kinds)], out_ref.at[place], sems.at[place]).wait()


def choose(pieces, received, which, start, kinds):
    shape = which.shape + (kinds,) + pieces.shape[1:]
    anywhere = pl.BlockSpec(memory_space=pl.ANY)
    return pl.pallas_call(
        functools.partial(choose_kernel, kinds),
        grid_spec=pltpu.PrefetchScalarGridSpec(
            num_scalar_prefetch=2,
            grid=(1,),
            in_specs=[anywhere] * (1 + len(received)),
            out_specs=pl.BlockSpec(shape, lambda i, *_: (0,) * len(shape)),
            scratch_shapes=[pltpu.SemaphoreType.DMA(which.shape)],
        ),
        out_shape=jax.ShapeDtypeStruct(shape, pieces.dtype),
        compiler_params=pltpu.CompilerParams(vmem_limit_bytes=VMEM_LIMIT),
        name="choose",
    )(which, start, pieces, *received)


def take(pieces, received, rest, plan):
    kinds = pieces.shape[0] // lax.axis_size("column")
    stays, late = plan["offset"] == 0, plan["rank"] >= FEW
    place = jnp.where(stays, plan["column"], jnp.where(late, plan["rank"] - FEW, plan["rank"]))
    which = jnp.where(stays | ~late, plan["offset"], plan["offset"] + len(received))
    return choose(pieces, [*received, *rest], which, place * kinds, kinds)


def rest_across(pieces, moments, plan):
    more = plan["by_shift"][:, FEW:]

    def send(pieces, moments):
        return send_planes(pieces, more), send_planes(moments, more)

    def skip(pieces, moments):
        empty = lambda array: [
            jnp.zeros((more.shape[1] * (array.shape[0] // lax.axis_size("column")),) + array.shape[1:], array.dtype)
        ] * more.shape[0]
        return empty(pieces), empty(moments)

    return lax.cond(plan["most"] >= FEW, send, skip, pieces, moments)


def local(
    attention_out,
    residual,
    upstream,
    norm_gain,
    weight,
    first_moment,
    second_moment,
    sources,
    rate_index,
):
    columns = lax.axis_size("column")
    minor = lax.axis_index("minor")
    depth, width = weight.shape[1:]
    rows = depth // columns
    features = residual.shape[2]

    gathered = lax.all_gather(attention_out[0], "major", axis=0, tiled=True)
    plan = plan_moves(sources)
    few = plan["by_shift"][:, :FEW]
    weights = spread_columns(weight[0].reshape(columns, rows, width))
    moments = jnp.stack(
        [array[0].reshape(columns, rows, width) for array in (first_moment, second_moment)], axis=1
    )
    stream = pack(residual[0], upstream[0], lax.axis_size("major"))
    weights, moments, stream = lax.optimization_barrier((weights, moments, stream))
    moments = spread_columns(moments).reshape(columns * (KINDS - 1), rows, width)
    weights_in = send_planes(weights, few)
    weights_in, moments = lax.optimization_barrier((weights_in, moments))
    weights_rest, moments_rest = rest_across(weights, moments, plan)
    weights = take(weights, weights_in, weights_rest, plan)
    weights, moments = lax.optimization_barrier((weights, moments))
    weights = spread_columns(weights.reshape(columns, rows, width))
    gain_other = swap_minor(norm_gain[0])
    gain = jnp.where(
        minor == 0,
        jnp.concatenate((norm_gain[0], gain_other)),
        jnp.concatenate((gain_other, norm_gain[0])),
    ).astype(jnp.float32)[None, :]
    weights, stream, gain = lax.optimization_barrier((weights, stream, gain))
    stream = lax.all_to_all(stream, "major", split_axis=0, concat_axis=0, tiled=True)
    weights = weights.reshape(depth, width)
    weights_other = swap_minor(weights)
    moments_in = send_planes(moments, few)

    inv_scale = 1.0 / math.sqrt(depth)
    side = minor.astype(jnp.int32)[None]
    hidden, sums = forward(side, gathered, weights, weights_other, gain, stream, inv_scale)
    moments, sums = lax.optimization_barrier((moments, sums))
    sums = sums_of_all(sums)
    moments = take(moments, moments_in, moments_rest, plan)
    moments, sums = lax.optimization_barrier((moments, sums))
    halves = backward(side, gathered, hidden, gain, sums, stream, inv_scale, features)
    moments, halves[0][0] = lax.optimization_barrier((moments, halves[0][0]))
    moments = spread_columns(moments)
    result = []
    for half, (mine, theirs) in enumerate(halves):
        result = adamw(half, rate_index, weights, moments, mine, swap_minor(theirs), result)
    return tuple(result)


def solution(mesh):
    members, shards = mesh.devices.shape
    split = Mesh(
        mesh.devices.reshape(PLANES, members // PLANES, shards // MINOR, MINOR),
        ("plane", "column", "major", "minor"),
    )
    member, fsdp = ("plane", "column"), ("major", "minor")
    in_specs = (
        P(member, fsdp, None),
        P(member, fsdp, None),
        P(member, fsdp, None),
        P(member, fsdp),
        P(member, None, fsdp),
        P(member, None, fsdp),
        P(member, None, fsdp),
        P(),
        P(member),
    )
    out_specs = (P(member, None, fsdp),) * 3
    return jax.shard_map(local, mesh=split, in_specs=in_specs, out_specs=out_specs, check_vma=False)
```

```python
import functools
import math

import jax
import jax.numpy as jnp
from jax import lax
from jax.experimental import pallas as pl
from jax.experimental.pallas import tpu as pltpu
from jax.sharding import Mesh
from jax.sharding import PartitionSpec as P

EPS = 1e-06
ADAM_EPS = 1e-08
BETA_ONE = 0.9
BETA_TWO = 0.95
DECAY = 0.1
bias_one = 1.0 - 0.9**10
bias_two = 1.0 - 0.95**10
RATE_TABLE = (0.02, 0.032, 0.05, 0.08, 0.125)
MINOR = 2
PLANES = 4
FEW = 2
LANES = 128
VMEM_LIMIT = 24 * 1024 * 1024
KINDS = 3
HALVES = 2


def adamw_kernel(rate_ref, weight_ref, moments_ref, mine_ref, theirs_ref, *refs):
    weight_out, first_out, second_out = refs[-3:]
    rate = jnp.float32(0.0)
    for slot, value in enumerate(RATE_TABLE):
        rate = jnp.where(rate_ref[0] == slot, jnp.float32(value), rate)
    gradient = mine_ref[...] + theirs_ref[...].astype(jnp.float32)
    weight_now = weight_ref[...].astype(jnp.float32)
    first_now = moments_ref[0, 0].astype(jnp.float32)
    second_now = moments_ref[0, 1].astype(jnp.float32)
    first_sum = BETA_ONE * first_now + (1.0 - BETA_ONE) * gradient
    second_sum = BETA_TWO * second_now + (1.0 - BETA_TWO) * gradient * gradient
    update = first_sum / bias_one / (jnp.sqrt(second_sum / bias_two) + ADAM_EPS)
    weight_new = weight_now * (1.0 - rate * DECAY) - rate * update
    weight_out[0] = weight_new.astype(jnp.bfloat16)
    first_out[0] = first_sum.astype(jnp.bfloat16)
    second_out[0] = second_sum.astype(jnp.bfloat16)


def adamw(half, rate_index, weight, moments, mine, theirs, earlier):
    pieces, _, rows, width = moments.shape
    steps = pieces // HALVES
    first = half * steps
    flat = pl.BlockSpec((rows, width), lambda i, r: (i, 0))
    out = pl.BlockSpec((1, rows, width), lambda i, r: (0, first + i, 0))
    count = len(earlier)
    return pl.pallas_call(
        adamw_kernel,
        grid_spec=pltpu.PrefetchScalarGridSpec(
            num_scalar_prefetch=1,
            grid=(steps,),
            in_specs=[
                pl.BlockSpec((rows, width), lambda i, r: (first + i, 0)),
                pl.BlockSpec((1, KINDS - 1, rows, width), lambda i, r: (first + i, 0, 0, 0)),
                flat,
                flat,
            ]
            + [pl.BlockSpec(memory_space=pl.ANY)] * count,
            out_specs=[out, out, out],
        ),
        out_shape=[jax.ShapeDtypeStruct((1, pieces * rows, width), jnp.bfloat16)] * KINDS,
        input_output_aliases={5 + i: i for i in range(count)},
        compiler_params=pltpu.CompilerParams(vmem_limit_bytes=VMEM_LIMIT),
        cost_estimate=pl.CostEstimate(
            flops=20 * steps * rows * width,
            bytes_accessed=18 * steps * rows * width,
            transcendentals=steps * rows * width,
        ),
        name="adamw",
    )(rate_index, weight, moments, mine, theirs, *earlier)


def pack_kernel(residual_ref, upstream_ref, out_ref):
    out_ref[0, 0] = residual_ref[...]
    out_ref[0, 1] = upstream_ref[...]


def pack(residual, upstream, blocks):
    tokens, features = residual.shape
    block = features // blocks
    columns = pl.BlockSpec((tokens, block), lambda i: (0, i))
    return pl.pallas_call(
        pack_kernel,
        grid=(blocks,),
        in_specs=[columns, columns],
        out_specs=pl.BlockSpec((1, 2, tokens, block), lambda i: (i, 0, 0, 0)),
        out_shape=jax.ShapeDtypeStruct((blocks, 2, tokens, block), residual.dtype),
        compiler_params=pltpu.CompilerParams(vmem_limit_bytes=VMEM_LIMIT),
        name="pack",
    )(residual, upstream)


def forward_kernel(inv_scale, side_ref, rows_ref, own_ref, other_ref, stream_ref, gain_ref, hidden_ref, sums_ref, both_ref):
    width = own_ref.shape[1]

    @pl.when(pl.program_id(0) == 0)
    def _():
        @pl.when(side_ref[0] == 0)
        def _():
            both_ref[:, :width] = own_ref[...]
            both_ref[:, width:] = other_ref[...]

        @pl.when(side_ref[0] != 0)
        def _():
            both_ref[:, :width] = other_ref[...]
            both_ref[:, width:] = own_ref[...]

    linear = jnp.dot(rows_ref[...], both_ref[...], preferred_element_type=jnp.float32)
    count, block = linear.shape
    stream = stream_ref[...]
    resid = stream[:, 0].reshape(count, block).astype(jnp.float32)
    upstream = stream[:, 1].reshape(count, block).astype(jnp.float32)
    hidden = resid + linear * inv_scale
    hidden_ref[...] = hidden
    scaled = upstream * gain_ref[...]
    squares = jnp.sum(hidden * hidden, axis=1, keepdims=True)
    inner = jnp.sum(scaled * hidden, axis=1, keepdims=True)
    lane = lax.broadcasted_iota(jnp.int32, (count, LANES), 1)
    packed = jnp.where(lane == 0, squares, jnp.where(lane == 1, inner, 0.0)).T[:2]
    for target in range(sums_ref.shape[0]):
        sums_ref[target] = packed


def forward(side, rows, own, other, gain, stream, inv_scale):
    tokens, depth = rows.shape
    blocks, _, per, block = stream.shape
    step = 2 * per
    return pl.pallas_call(
        functools.partial(forward_kernel, inv_scale),
        grid_spec=pltpu.PrefetchScalarGridSpec(
            num_scalar_prefetch=1,
            grid=(tokens // step,),
            in_specs=[
                pl.BlockSpec((step, depth), lambda i, m: (i, 0)),
                pl.BlockSpec(own.shape, lambda i, m: (0, 0)),
                pl.BlockSpec(other.shape, lambda i, m: (0, 0)),
                pl.BlockSpec((2, 2, per, block), lambda i, m: (i, 0, 0, 0)),
                pl.BlockSpec(gain.shape, lambda i, m: (0, 0)),
            ],
            out_specs=[
                pl.BlockSpec((step, block), lambda i, m: (i, 0)),
                pl.BlockSpec((blocks, 2, step), lambda i, m: (0, 0, i)),
            ],
            scratch_shapes=[pltpu.VMEM((depth, block), jnp.bfloat16)],
        ),
        out_shape=[
            jax.ShapeDtypeStruct((tokens, block), jnp.float32),
            jax.ShapeDtypeStruct((blocks, 2, tokens), jnp.float32),
        ],
        compiler_params=pltpu.CompilerParams(vmem_limit_bytes=VMEM_LIMIT),
        cost_estimate=pl.CostEstimate(
            flops=2 * tokens * depth * block, bytes_accessed=7 * 1024 * 1024, transcendentals=0
        ),
        name="forward",
    )(side, rows, own, other, stream, gain)


def multiply(inv_scale, side_ref, delta, rows_ref, mine_ref, theirs_ref):
    width = mine_ref.shape[1]
    grad = jnp.dot(delta, rows_ref[...], preferred_element_type=jnp.float32) * inv_scale
    low = grad[:width].T
    high = grad[width:].T
    first = side_ref[0] == 0
    mine_ref[...] = jnp.where(first, low, high)
    theirs_ref[...] = jnp.where(first, high, low).astype(jnp.bfloat16)


def backward_first_kernel(inv_scale, features, side_ref, rows_ref, hidden_ref, gain_ref, sums_ref, stream_ref, mine_ref, theirs_ref, delta_ref):
    width = mine_ref.shape[1]
    blocks, _, per, _ = stream_ref.shape

    @pl.when(pl.program_id(0) == 0)
    def _():
        sums = jnp.sum(sums_ref[...], axis=0)
        inverse = lax.rsqrt(sums[0:1] / features + EPS)
        factor = sums[1:2] / features * (inverse * inverse * inverse)
        for block in range(blocks):
            place = slice(block * per, (block + 1) * per)
            inverse_here = jnp.broadcast_to(inverse[:, place], (LANES, per)).T
            factor_here = jnp.broadcast_to(factor[:, place], (LANES, per)).T
            for half in range(2):
                cols = slice(half * width, (half + 1) * width)
                scaled = stream_ref[block, 1, :, cols].astype(jnp.float32) * gain_ref[:, cols]
                delta = scaled * inverse_here - hidden_ref[place, cols] * factor_here
                delta_ref[cols, place] = delta.T.astype(jnp.bfloat16)

    multiply(inv_scale, side_ref, delta_ref[...], rows_ref, mine_ref, theirs_ref)


def backward_next_kernel(inv_scale, side_ref, rows_ref, delta_ref, mine_ref, theirs_ref):
    multiply(inv_scale, side_ref, delta_ref[...], rows_ref, mine_ref, theirs_ref)


def backward(side, rows, hidden, gain, sums, stream, inv_scale, features):
    tokens, depth = rows.shape
    block = hidden.shape[1]
    width = block // 2
    step = 256
    steps = depth // step // HALVES
    params = pltpu.CompilerParams(vmem_limit_bytes=VMEM_LIMIT)
    cost = pl.CostEstimate(
        flops=2 * tokens * depth * block // HALVES, bytes_accessed=5 * 1024 * 1024, transcendentals=0
    )
    outs = [
        jax.ShapeDtypeStruct((depth // HALVES, width), jnp.float32),
        jax.ShapeDtypeStruct((depth // HALVES, width), jnp.bfloat16),
    ]
    whole = lambda array: pl.BlockSpec(array.shape, lambda i, *_: (0,) * array.ndim)
    delta = jax.ShapeDtypeStruct((block, tokens), jnp.bfloat16)
    out = pl.BlockSpec((step, width), lambda i, *_: (i, 0))
    *first, delta = pl.pallas_call(
        functools.partial(backward_first_kernel, inv_scale, features),
        grid_spec=pltpu.PrefetchScalarGridSpec(
            num_scalar_prefetch=1,
            grid=(steps,),
            in_specs=[pl.BlockSpec((tokens, step), lambda i, *_: (0, i))]
            + [whole(array) for array in (hidden, gain, sums, stream)],
            out_specs=[out, out, whole(delta)],
        ),
        out_shape=outs + [delta],
        compiler_params=params,
        cost_estimate=cost,
        name="backward_first",
    )(side, rows, hidden, gain, sums, stream)
    result = [first]
    for half in range(1, HALVES):
        result.append(
            pl.pallas_call(
                functools.partial(backward_next_kernel, inv_scale),
                grid_spec=pltpu.PrefetchScalarGridSpec(
                    num_scalar_prefetch=1,
                    grid=(steps,),
                    in_specs=[
                        pl.BlockSpec((tokens, step), lambda i, *_, half=half: (0, half * steps + i)),
                        whole(delta),
                    ],
                    out_specs=[out, out],
                ),
                out_shape=outs,
                compiler_params=params,
                cost_estimate=cost,
                name="backward_next",
            )(side, rows, delta)
        )
    return result


def swap_minor(array):
    return lax.ppermute(array, "minor", [(0, 1), (1, 0)])


def sums_of_all(sums):
    return lax.all_to_all(sums, "major", split_axis=0, concat_axis=0, tiled=True)


def spread_columns(array):
    return lax.all_to_all(array, "column", split_axis=0, concat_axis=0, tiled=True)


def plan_moves(sources):
    planes = lax.axis_size("plane")
    columns = lax.axis_size("column")
    me = lax.axis_index("plane")
    member = jnp.arange(planes * columns, dtype=jnp.int32)
    here, there = member // columns, sources // columns
    offset = lax.rem(here - there + planes, planes)
    earlier = member[None, :] < member[:, None]
    same = (here[None, :] == here[:, None]) & (there[None, :] == there[:, None])
    rank = jnp.sum((earlier & same).astype(jnp.int32), axis=1)
    most = jnp.max(jnp.where(offset > 0, rank, 0))
    targets = jnp.arange(1, planes, dtype=jnp.int32)[:, None, None]
    slots = jnp.arange(columns, dtype=jnp.int32)[None, :, None]
    leaving = (there == me) & (rank == slots)
    column = lax.rem(sources, columns)
    by_shift = jnp.sum(jnp.where(leaving & (offset == targets), column, 0), axis=2)
    mine = lambda values: lax.dynamic_slice_in_dim(values, me * columns, columns)
    return dict(
        column=mine(column),
        offset=mine(offset),
        rank=mine(rank),
        by_shift=by_shift,
        most=most,
    )


def pick(pieces, slots):
    kinds = pieces.shape[0] // lax.axis_size("column")
    return pieces[(slots[:, None] * kinds + jnp.arange(kinds, dtype=jnp.int32)).reshape(-1)]


def send_plane(pieces, slots, shift):
    planes = lax.axis_size("plane")
    return lax.ppermute(pick(pieces, slots[shift - 1]), "plane", [(i, (i + shift) % planes) for i in range(planes)])


def send_planes(pieces, slots):
    return [send_plane(pieces, slots, shift) for shift in range(1, lax.axis_size("plane"))]


def choose_kernel(kinds, which_ref, start_ref, *refs):
    refs, out_ref, sems = refs[:-2], refs[-2], refs[-1]
    columns = out_ref.shape[0]
    for place in range(columns):
        for number, ref in enumerate(refs):
            @pl.when(which_ref[place] == number)
            def _():
                source = ref.at[pl.ds(start_ref[place], kinds)]
                pltpu.make_async_copy(source, out_ref.at[place], sems.at[place]).start()

    for place in range(columns):
        pltpu.make_async_copy(refs[0].at[pl.ds(0, kinds)], out_ref.at[place], sems.at[place]).wait()


def choose(pieces, received, which, start, kinds):
    shape = which.shape + (kinds,) + pieces.shape[1:]
    anywhere = pl.BlockSpec(memory_space=pl.ANY)
    return pl.pallas_call(
        functools.partial(choose_kernel, kinds),
        grid_spec=pltpu.PrefetchScalarGridSpec(
            num_scalar_prefetch=2,
            grid=(1,),
            in_specs=[anywhere] * (1 + len(received)),
            out_specs=pl.BlockSpec(shape, lambda i, *_: (0,) * len(shape)),
            scratch_shapes=[pltpu.SemaphoreType.DMA(which.shape)],
        ),
        out_shape=jax.ShapeDtypeStruct(shape, pieces.dtype),
        compiler_params=pltpu.CompilerParams(vmem_limit_bytes=VMEM_LIMIT),
        name="choose",
    )(which, start, pieces, *received)


def take(pieces, received, rest, plan):
    kinds = pieces.shape[0] // lax.axis_size("column")
    stays, late = plan["offset"] == 0, plan["rank"] >= FEW
    place = jnp.where(stays, plan["column"], jnp.where(late, plan["rank"] - FEW, plan["rank"]))
    which = jnp.where(stays | ~late, plan["offset"], plan["offset"] + len(received))
    return choose(pieces, [*received, *rest], which, place * kinds, kinds)


def rest_across(pieces, moments, plan):
    more = plan["by_shift"][:, FEW:]

    def send(pieces, moments):
        return send_planes(pieces, more), send_planes(moments, more)

    def skip(pieces, moments):
        shapes = [
            jax.ShapeDtypeStruct(
                (more.shape[1] * (array.shape[0] // lax.axis_size("column")),) + array.shape[1:], array.dtype
            )
            for array in (pieces, moments)
            for _ in range(more.shape[0])
        ]
        unused = pl.pallas_call(
            lambda *refs: None,
            out_specs=[pl.BlockSpec(memory_space=pl.ANY)] * len(shapes),
            out_shape=shapes,
            name="unused",
        )()
        return list(unused[: more.shape[0]]), list(unused[more.shape[0] :])

    return lax.cond(plan["most"] >= FEW, send, skip, pieces, moments)


def local(
    attention_out,
    residual,
    upstream,
    norm_gain,
    weight,
    first_moment,
    second_moment,
    sources,
    rate_index,
):
    columns = lax.axis_size("column")
    minor = lax.axis_index("minor")
    depth, width = weight.shape[1:]
    rows = depth // columns
    features = residual.shape[2]

    gathered = lax.all_gather(attention_out[0], "major", axis=0, tiled=True)
    plan = plan_moves(sources)
    few = plan["by_shift"][:, :FEW]
    weights = spread_columns(weight[0].reshape(columns, rows, width))
    moments = jnp.stack(
        [array[0].reshape(columns, rows, width) for array in (first_moment, second_moment)], axis=1
    )
    stream = pack(residual[0], upstream[0], lax.axis_size("major"))
    weights, moments, stream = lax.optimization_barrier((weights, moments, stream))
    moments = spread_columns(moments).reshape(columns * (KINDS - 1), rows, width)
    weights_in = send_planes(weights, few)
    weights_in, moments = lax.optimization_barrier((weights_in, moments))
    weights_rest, moments_rest = rest_across(weights, moments, plan)
    weights = take(weights, weights_in, weights_rest, plan)
    weights, moments = lax.optimization_barrier((weights, moments))
    weights = spread_columns(weights.reshape(columns, rows, width))
    gain_other = swap_minor(norm_gain[0])
    gain = jnp.where(
        minor == 0,
        jnp.concatenate((norm_gain[0], gain_other)),
        jnp.concatenate((gain_other, norm_gain[0])),
    ).astype(jnp.float32)[None, :]
    weights, stream, gain = lax.optimization_barrier((weights, stream, gain))
    stream = lax.all_to_all(stream, "major", split_axis=0, concat_axis=0, tiled=True)
    weights = weights.reshape(depth, width)
    weights_other = swap_minor(weights)
    moments_in = send_planes(moments, few)

    inv_scale = 1.0 / math.sqrt(depth)
    side = minor.astype(jnp.int32)[None]
    hidden, sums = forward(side, gathered, weights, weights_other, gain, stream, inv_scale)
    moments, sums = lax.optimization_barrier((moments, sums))
    sums = sums_of_all(sums)
    moments = take(moments, moments_in, moments_rest, plan)
    moments, sums = lax.optimization_barrier((moments, sums))
    moments = spread_columns(moments)
    halves = backward(side, gathered, hidden, gain, sums, stream, inv_scale, features)
    result = []
    for half, (mine, theirs) in enumerate(halves):
        result = adamw(half, rate_index, weights, moments, mine, swap_minor(theirs), result)
    return tuple(result)


def solution(mesh):
    members, shards = mesh.devices.shape
    split = Mesh(
        mesh.devices.reshape(PLANES, members // PLANES, shards // MINOR, MINOR),
        ("plane", "column", "major", "minor"),
    )
    member, fsdp = ("plane", "column"), ("major", "minor")
    in_specs = (
        P(member, fsdp, None),
        P(member, fsdp, None),
        P(member, fsdp, None),
        P(member, fsdp),
        P(member, None, fsdp),
        P(member, None, fsdp),
        P(member, None, fsdp),
        P(),
        P(member),
    )
    out_specs = (P(member, None, fsdp),) * 3
    return jax.shard_map(local, mesh=split, in_specs=in_specs, out_specs=out_specs, check_vma=False)
```
